32 devices in a mesh: dp: 8 (over z, y), tier: 2 (over core), head: 2 (over x).
Axes of the slice: x: 2, y: 2, z: 4, core: 2. Of those that a mesh axis runs over, the one named last changes fastest.
Arguments:
- segment_input: bfloat16 [24, 512, 1024], P('dp', 'tier'), may hold values from -6 to 6
- memory: bfloat16 [24, 512, 1024], P('dp', 'tier'), may hold values from -6 to 6
- compressed: bfloat16 [24, 384, 1024], P('dp', 'tier'), may hold values from -6 to 6
- evicted: bfloat16 [24, 384, 1024], P('dp', 'tier'), may hold values from -6 to 6
- cotangent: bfloat16 [24, 512, 1024], P('dp', 'tier'), may hold values from -6 to 6
- seg_lengths: int32 [24], P('dp'), may hold values from 128 to 512, as said below
- memory_fills: int32 [24], P('dp'), may hold values from 0 to 512, as said below
- compressed_fills: int32 [24], P('dp'), may hold values from 1 to 512, as said below
- conv_weight: bfloat16 [3, 1024, 1024], P(None, ('dp', 'tier'), 'head'), may hold values from -0.109375 to 0.109375
- conv_bias: float32 [1024], P('head'), may hold values from -1.75 to 1.75
- norm1_gain: float32 [1024], replicated, may hold values from 0.5 to 1.5
- norm1_bias: float32 [1024], replicated, may hold values from -1.25 to 1.25
- query_weight: bfloat16 [1024, 1024], P(('dp', 'tier'), 'head'), may hold values from -0.1875 to 0.1875
- key_weight: bfloat16 [1024, 1024], P(('dp', 'tier'), 'head'), may hold values from -0.1875 to 0.1875
- value_weight: bfloat16 [1024, 1024], P(('dp', 'tier'), 'head'), may hold values from -0.1875 to 0.1875
- position_weight: bfloat16 [1024, 1024], P(('dp', 'tier'), 'head'), may hold values from -0.1875 to 0.1875
- content_bias: float32 [8, 128], P('head'), may hold values from -3 to 3
- position_bias: float32 [8, 128], P('head'), may hold values from -3 to 3
- out_weight: bfloat16 [1024, 1024], P('head', ('dp', 'tier')), may hold values from -2 to 2
- norm2_gain: float32 [1024], replicated, may hold values from 0.5 to 1.5
- norm2_bias: float32 [1024], replicated, may hold values from -1.25 to 1.25
- up_weight: bfloat16 [1024, 4096], P(('dp', 'tier'), 'head'), may hold values from -0.1875 to 0.1875
- up_bias: float32 [4096], P('head'), may hold values from -1.75 to 1.75
- down_weight: bfloat16 [4096, 1024], P('head', ('dp', 'tier')), may hold values from -0.09375 to 0.09375
- down_bias: float32 [1024], replicated, may hold values from -1.75 to 1.75
Outputs:
- output: bfloat16 [24, 512, 1024], P('dp', 'tier')
- grad_input: float32 [24, 512, 1024], P('dp', 'tier')
- grad_compressed: float32 [24, 384, 1024], P('dp', 'tier')
- grad_conv_weight: float32 [3, 1024, 1024], P(None, ('dp', 'tier'), 'head')
- grad_conv_bias: float32 [1024], P('head')
- grad_norm1_gain: float32 [1024], replicated
- grad_norm1_bias: float32 [1024], replicated
- grad_query_weight: float32 [1024, 1024], P(('dp', 'tier'), 'head')
- grad_key_weight: float32 [1024, 1024], P(('dp', 'tier'), 'head')
- grad_value_weight: float32 [1024, 1024], P(('dp', 'tier'), 'head')
- grad_position_weight: float32 [1024, 1024], P(('dp', 'tier'), 'head')
- grad_content_bias: float32 [8, 128], P('head')
- grad_position_bias: float32 [8, 128], P('head')
- grad_out_weight: float32 [1024, 1024], P('head', ('dp', 'tier'))
- grad_norm2_gain: float32 [1024], replicated
- grad_norm2_bias: float32 [1024], replicated
- grad_up_weight: float32 [1024, 4096], P(('dp', 'tier'), 'head')
- grad_up_bias: float32 [4096], P('head')
- grad_down_weight: float32 [4096, 1024], P('head', ('dp', 'tier'))
- grad_down_bias: float32 [1024], replicated
The draws below stay inside these ranges and needn't reach their ends.
Inputs may be any that keep to these rules, and one draw needn't show every extreme that they name: `seg_lengths`: tokens of a stream's segment that are real; later positions are padding. `memory_fills`: how many of a stream's newest memory rows hold data; older ones are empty. `compressed_fills`: how many of a stream's newest compressed rows (the 128 fresh ones last) hold data.
All inputs are finite; a program needn't handle non-finite values.
Results may differ from the reference program's by a relative error of at most 0.035.
Values may be sent and summed in bfloat16 or wider, within the bound.
No kernel may reach another device: no remote copies, remote signals or barrier semaphores. Data moves between devices by JAX's collectives and lax.ppermute only.
A program may use at most 160 MiB of HBM per device.

```python
import math
import jax
import jax.numpy as jnp
from jax import lax

D = 1024
HEADS = 8
HDIM = 128
FF = 4096
SEG = 512
MEM = 512
CMEM = 512
NEWC = 128
KW = 3
STREAMS = 24
OLDC = 384
EVICT = 384


def ragged_counts(key, salt, lowest, highest):
    salted = jax.random.fold_in(key, salt)
    split_keys = jax.random.split(salted, 2)
    short_len = jax.random.randint(split_keys[0], (STREAMS,), lowest, highest)
    full_pick = jax.random.randint(split_keys[1], (STREAMS,), 0, 4) > 0
    counts_drawn = jnp.where(full_pick, highest, short_len)
    return counts_drawn.at[0].set(highest).astype(jnp.int32)


def draw_seg_lengths(key, part):
    return ragged_counts(key, 101, SEG // 4, SEG)


def draw_memory_fills(key, part):
    return ragged_counts(key, 202, 0, MEM)


def draw_compressed_fills(key, part):
    return ragged_counts(key, 303, 1, CMEM)


def drawn_rows(key, rows):
    return jnp.clip(jax.random.normal(key, (STREAMS, rows, D), jnp.float32), -6.0, 6.0)


def draw_segment_input(key, part):
    key = jax.random.fold_in(key, 11)
    return drawn_rows(key, SEG).astype(jnp.bfloat16)


def draw_memory(key, part):
    key = jax.random.fold_in(key, 12)
    return drawn_rows(key, MEM).astype(jnp.bfloat16)


def draw_compressed(key, part):
    key = jax.random.fold_in(key, 13)
    return drawn_rows(key, OLDC).astype(jnp.bfloat16)


def draw_evicted(key, part):
    key = jax.random.fold_in(key, 14)
    return drawn_rows(key, EVICT).astype(jnp.bfloat16)


def shard_levels(key, shape, shards, low, high):
    level = 1.0
    for position, blocks in shards:
        steps = jax.random.uniform(jax.random.fold_in(jax.random.fold_in(key, 6), position), (blocks,), jnp.float32, low / len(shards), high / len(shards))
        level = level * jnp.repeat(jnp.exp(steps), shape[position] // blocks).reshape((-1,) + (1,) * (len(shape) - 1 - position))
    return level


def gaussian(key, extent, scale, limit, cuts=(), held_as=jnp.bfloat16):
    loudness = shard_levels(key, extent, cuts, -0.22, 0.18) if cuts else 1.0
    array = jax.random.normal(key, extent, jnp.float32) * scale * loudness
    return jnp.minimum(jnp.maximum(array, -limit), limit).astype(held_as)


def setup_inputs(seed: int = 0) -> dict:
    seeds = jax.random.split(jax.random.key(seed), 26)
    return {
        "segment_input": draw_segment_input(jax.random.fold_in(seeds[25], 71), 0),
        "memory": draw_memory(jax.random.fold_in(seeds[25], 71), 0),
        "compressed": draw_compressed(jax.random.fold_in(seeds[25], 71), 0),
        "evicted": draw_evicted(jax.random.fold_in(seeds[25], 71), 0),
        "cotangent": gaussian(seeds[4], (STREAMS, SEG, D), 1.0, 6.0, ((0, 8), (1, 2))),
        "seg_lengths": draw_seg_lengths(jax.random.fold_in(seeds[25], 71), 0),
        "memory_fills": draw_memory_fills(jax.random.fold_in(seeds[25], 71), 0),
        "compressed_fills": draw_compressed_fills(jax.random.fold_in(seeds[25], 71), 0),
        "conv_weight": gaussian(seeds[8], (KW, D, D), (KW * D) ** -0.5, 0.109375, ((1, 16), (2, 2))),
        "conv_bias": gaussian(seeds[9], (D,), 0.3, 1.75, ((0, 2),), jnp.float32),
        "norm1_gain": jnp.clip(1.0 + 0.1 * jax.random.normal(seeds[10], (D,), jnp.float32), 0.5, 1.5),
        "norm1_bias": gaussian(seeds[11], (D,), 0.2, 1.25, (), jnp.float32),
        "query_weight": gaussian(seeds[12], (D, HEADS * HDIM), D ** -0.5, 0.1875, ((0, 16), (1, 2))),
        "key_weight": gaussian(seeds[13], (D, HEADS * HDIM), D ** -0.5, 0.1875, ((0, 16), (1, 2))),
        "value_weight": gaussian(seeds[14], (D, HEADS * HDIM), D ** -0.5, 0.1875, ((0, 16), (1, 2))),
        "position_weight": gaussian(seeds[15], (D, HEADS * HDIM), D ** -0.5, 0.1875, ((0, 16), (1, 2))),
        "content_bias": gaussian(seeds[16], (HEADS, HDIM), 0.5, 3.0, ((0, 2),), jnp.float32),
        "position_bias": gaussian(seeds[17], (HEADS, HDIM), 0.5, 3.0, ((0, 2),), jnp.float32),
        "out_weight": gaussian(seeds[18], (HEADS * HDIM, D), (HEADS * HDIM // 128) ** -0.5, 2.0, ((0, 2), (1, 16))),
        "norm2_gain": jnp.clip(1.0 + 0.1 * jax.random.normal(seeds[19], (D,), jnp.float32), 0.5, 1.5),
        "norm2_bias": gaussian(seeds[20], (D,), 0.2, 1.25, (), jnp.float32),
        "up_weight": gaussian(seeds[21], (D, FF), D ** -0.5, 0.1875, ((0, 16), (1, 2))),
        "up_bias": gaussian(seeds[22], (FF,), 0.3, 1.75, ((0, 2),), jnp.float32),
        "down_weight": gaussian(seeds[23], (FF, D), FF ** -0.5, 0.09375, ((0, 2), (1, 16))),
        "down_bias": gaussian(seeds[24], (D,), 0.3, 1.75, (), jnp.float32),
    }


norm_eps = 1e-05
neg_fill = -1e+30

@jax.custom_vjp
def low(v):
    return lax.optimization_barrier(v.astype(jnp.bfloat16)).astype(jnp.float32)

@jax.custom_vjp
def low_back(v):
    return v

def low_keep(v):
    return (low(v), None)

def low_pass(kept, grad):
    return (grad,)

def back_keep(v):
    return (v, None)

def back_low(kept, grad):
    return (low(grad),)
low.defvjp(low_keep, low_pass)
low_back.defvjp(back_keep, back_low)

def smooth_gate(values_in):
    return jax.nn.gelu(values_in, approximate=True)

def matmul_high(left_mat, right_mat):
    return jnp.dot(left_mat, right_mat, precision=lax.Precision.HIGHEST, preferred_element_type=jnp.float32)

def layer_norm(row_vals, gain_vec, shift_vec):
    row_mean = lax.optimization_barrier(jnp.mean(row_vals, axis=-1, keepdims=True))
    centred = row_vals - row_mean
    row_var = lax.optimization_barrier(jnp.mean(centred * centred, axis=-1, keepdims=True))
    return centred * lax.rsqrt(row_var + norm_eps) * gain_vec + shift_vec

def sin_cos(positions):
    half_width = D // 2
    frequency = jnp.exp(jnp.arange(half_width, dtype=jnp.float32) * (-2.0 * math.log(10000.0) / D))
    turned = positions.astype(jnp.float32)[:, None] * frequency[None, :]
    return (jnp.sin(turned), jnp.cos(turned))

def rotate(amplitude, sin_rows, cos_rows):
    half_width = amplitude.shape[-1] // 2
    sin_part = amplitude[..., :half_width]
    cos_part = amplitude[..., half_width:]
    return jnp.concatenate([sin_part * sin_rows + cos_part * cos_rows, cos_part * sin_rows - sin_part * cos_rows], axis=-1)

def key_valid(key_pos, query_pos, seg_len, mem_fill, comp_fill):
    query_start = CMEM + MEM
    in_comp = key_pos < CMEM
    in_memory = key_pos < query_start
    comp_ok = key_pos >= CMEM - comp_fill
    memory_ok = key_pos >= query_start - mem_fill
    seg_index = key_pos - query_start
    seg_ok = (seg_index < seg_len) & (seg_index <= query_pos[:, None])
    return jnp.where(in_comp, comp_ok, jnp.where(in_memory, memory_ok, seg_ok))

def stream_forward(params, input_rows, comp_rows, memory_rows, evicted_rows, seg_len, mem_fill, comp_fill):
    conv_w, conv_b, gain_one, shift_one, query_w, key_matrix, value_matrix, pos_w, content_b, pos_b, out_w, gain_two, shift_two, up_w, up_b, down_w, down_b = params
    scale_factor = 1.0 / math.sqrt(HDIM)
    grouped = evicted_rows.reshape(NEWC, KW * D)
    fresh_rows = low_back(low(matmul_high(grouped, conv_w.reshape(KW * D, D)) + conv_b))
    context = jnp.concatenate([comp_rows, fresh_rows, memory_rows, input_rows], axis=0)
    key_count = context.shape[0]
    query_start = CMEM + MEM
    normed = low(layer_norm(context, gain_one, shift_one))
    queries = low_back(low(matmul_high(normed[query_start:], query_w)))
    key_projection = low_back(low(matmul_high(normed, key_matrix)))
    value_proj = low_back(low(matmul_high(normed, value_matrix)))
    with_content = low(queries + content_b.reshape(-1))
    with_pos = low(queries + pos_b.reshape(-1))
    content_heads = with_content.reshape(SEG, HEADS, HDIM)
    position_heads = with_pos.reshape(SEG, HEADS, HDIM)
    key_heads = key_projection.reshape(key_count, HEADS, HDIM)
    value_heads = value_proj.reshape(key_count, HEADS, HDIM)
    pos_matrix = pos_w.reshape(D, HEADS, HDIM)
    amplitude = jnp.einsum('ihe,fhe->hif', position_heads, pos_matrix, precision=lax.Precision.HIGHEST)
    query_pos = jnp.arange(SEG, dtype=jnp.int32)
    key_pos = jnp.arange(key_count, dtype=jnp.int32)
    sin_query, cos_query = sin_cos(query_pos + query_start)
    sin_key, cos_key = sin_cos(key_pos)
    rotated = low(rotate(amplitude, sin_query, cos_query))
    key_table = low(jnp.concatenate([cos_key, sin_key], axis=-1))
    content = jnp.einsum('ihe,jhe->hij', content_heads, key_heads, precision=lax.Precision.HIGHEST)
    relative = jnp.einsum('hif,jf->hij', rotated, key_table, precision=lax.Precision.HIGHEST)
    scores = low_back((content + relative) * scale_factor)
    allowed = key_valid(key_pos, query_pos, seg_len, mem_fill, comp_fill)
    masked = jnp.where(allowed[None], scores, neg_fill)
    weights = low(jax.nn.softmax(masked, axis=-1))
    attended = jnp.einsum('hij,jhe->ihe', weights, value_heads, precision=lax.Precision.HIGHEST)
    attended = low_back(low(attended.reshape(SEG, HEADS * HDIM)))
    branch = low_back(matmul_high(attended, out_w))
    hidden_one = input_rows + branch
    normed_two = low(layer_norm(hidden_one, gain_two, shift_two))
    pre_act = low_back(matmul_high(normed_two, up_w) + up_b)
    activated = low(smooth_gate(pre_act))
    ffn_out = low_back(matmul_high(activated, down_w) + down_b)
    return hidden_one + ffn_out

def reference(segment_input, memory, compressed, evicted, cotangent, seg_lengths, memory_fills, compressed_fills, conv_weight, conv_bias, norm1_gain, norm1_bias, query_weight, key_weight, value_weight, position_weight, content_bias, position_bias, out_weight, norm2_gain, norm2_bias, up_weight, up_bias, down_weight, down_bias):
    params = tuple((param_item.astype(jnp.float32) for param_item in (conv_weight, conv_bias, norm1_gain, norm1_bias, query_weight, key_weight, value_weight, position_weight, content_bias, position_bias, out_weight, norm2_gain, norm2_bias, up_weight, up_bias, down_weight, down_bias)))
    zero_grads = tuple((jnp.zeros_like(param_item) for param_item in params))

    def one_stream(totals, stream_items):
        input_rows, comp_rows, memory_rows, evicted_rows, cot_rows, seg_len, mem_fill, comp_fill = stream_items
        live_rows = (jnp.arange(SEG, dtype=jnp.int32) < seg_len).astype(jnp.float32)

        def closed(param_set, input_in, comp_in):
            return stream_forward(param_set, input_in, comp_in, memory_rows, evicted_rows, seg_len, mem_fill, comp_fill)
        output, pull_back = jax.vjp(closed, params, input_rows, comp_rows)
        grad_params, grad_in, grad_comp = pull_back(cot_rows * live_rows[:, None])
        totals = tuple((left_item + right_item for left_item, right_item in zip(totals, grad_params)))
        return (totals, (output.astype(jnp.bfloat16), grad_in, grad_comp))
    totals, (outputs, grad_input, grad_comp) = lax.scan(one_stream, zero_grads, (segment_input.astype(jnp.float32), compressed.astype(jnp.float32), memory.astype(jnp.float32), evicted.astype(jnp.float32), cotangent.astype(jnp.float32), seg_lengths, memory_fills, compressed_fills))
    return (outputs, grad_input, grad_comp, totals[0], totals[1], totals[2], totals[3], totals[4], totals[5], totals[6], totals[7], totals[8], totals[9], totals[10], totals[11], totals[12], totals[13], totals[14], totals[15], totals[16])
```

```python
import functools
import math

import jax
import jax.numpy as jnp
import ml_dtypes
import numpy as np
from jax import lax
from jax.experimental import pallas as pl
from jax.experimental.pallas import tpu as pltpu
from jax.sharding import PartitionSpec as P

D = 1024
MEM = 512
CMEM = 512
KW = 3
OLDC = 384
EPS = 1e-05
NEG = -1e30
F32 = jnp.float32
BF16 = jnp.bfloat16


def swap(x, axis, step=1):
    n = lax.axis_size(axis)
    return lax.ppermute(x, axis, [(i, i ^ step) for i in range(n)])


def turn(x, steps):
    n = lax.axis_size("dp")
    zn = n // 2
    return lax.ppermute(
        x, "dp", [(i, ((i // 2 + steps) % zn) * 2 + i % 2) for i in range(n)]
    )


def head_sum(x):
    if lax.axis_size("head") == 2:
        return x.astype(F32) + swap(x, "head").astype(F32)
    return lax.psum(x, "head").astype(F32)


def head_gather(x):
    if lax.axis_size("head") == 2:
        other = swap(x, "head")
        first = lax.axis_index("head") == 0
        return jnp.concatenate(
            [jnp.where(first, x, other), jnp.where(first, other, x)], axis=-1
        )
    return lax.all_gather(x, "head", axis=x.ndim - 1, tiled=True)


def place_kernel(zn, rows, at_ref, *refs):
    count = zn * 4
    blocks, out, sems = refs[:count], refs[count], refs[count + 1]
    z, y, t = at_ref[0], at_ref[1], at_ref[2]
    copies = []
    for k in range(count):
        turned, flip_y, flip_t = k % zn, (k // zn) % 2, k // (2 * zn)
        zz = lax.rem(z + zn - turned, zn)
        yy = y + flip_y - 2 * y * flip_y
        tt = t + flip_t - 2 * t * flip_t
        row = pl.multiple_of(((zz * 2 + yy) * 2 + tt) * rows, rows)
        copies.append(
            pltpu.make_async_copy(blocks[k], out.at[pl.ds(row, rows)], sems.at[k])
        )
    for copy in copies:
        copy.start()
    for copy in copies:
        copy.wait()


def gather_rows(x):
    n = lax.axis_size("dp")
    rows, cols = x.shape
    zn = n // 2
    ring = [x] + [turn(x, s) for s in range(1, zn)]
    own = ring + [swap(r, "dp") for r in ring]
    blocks = own + [swap(r, "tier") for r in own]
    dp = lax.axis_index("dp")
    at = jnp.stack([dp // 2, dp % 2, lax.axis_index("tier")]).astype(jnp.int32)
    return pl.pallas_call(
        functools.partial(place_kernel, zn, rows),
        grid_spec=pltpu.PrefetchScalarGridSpec(
            num_scalar_prefetch=1,
            grid=(1,),
            in_specs=[pl.BlockSpec(memory_space=pl.ANY)] * len(blocks),
            out_specs=pl.BlockSpec((n * 2 * rows, cols), lambda i, s: (0, 0)),
            scratch_shapes=[pltpu.SemaphoreType.DMA((len(blocks),))],
        ),
        out_shape=jax.ShapeDtypeStruct((n * 2 * rows, cols), x.dtype),
        compiler_params=pltpu.CompilerParams(vmem_limit_bytes=48 << 20),
        name="place",
    )(at, *blocks)


def reduce_rows(g):
    n = lax.axis_size("dp")
    zn = n // 2
    dp = lax.axis_index("dp")
    z, y, t = dp // 2, dp % 2, lax.axis_index("tier")
    rows = g.shape[0] // (n * 2)

    def pick(v, k, axis):
        return lax.dynamic_index_in_dim(v, k, axis, keepdims=False)

    v = g.reshape(zn, 2, 2, rows, -1)
    v = (
        pick(v, t, 2).astype(F32) + swap(pick(v, 1 - t, 2), "tier").astype(F32)
    ).astype(BF16)
    v = (pick(v, y, 1).astype(F32) + swap(pick(v, 1 - y, 1), "dp").astype(F32)).astype(
        BF16
    )
    total = pick(v, z, 0).astype(F32)
    for s in range(1, zn):
        total = total + turn(pick(v, lax.rem(z + s, zn), 0), s).astype(F32)
    return total


def small_sum(parts):
    flat = jnp.concatenate([p.reshape(-1) for p in parts])
    pad = -flat.shape[0] % 1024
    flat = jnp.pad(flat, (0, pad)).reshape(-1, 128)
    n = lax.axis_size("dp")
    if n & (n - 1):
        flat = lax.psum(flat, ("dp", "tier"))
    else:
        flat = flat + swap(flat, "tier")
        step = 1
        while step < n:
            flat = flat + swap(flat, "dp", step)
            step *= 2
    flat = flat.reshape(-1)
    out, at = [], 0
    for p in parts:
        out.append(flat[at : at + p.size].reshape(p.shape))
        at += p.size
    return out


def dot(a, b, contract):
    return lax.dot_general(a, b, (contract, ((), ())), preferred_element_type=F32)


def key_pieces(sizes):
    comp, fresh, mem, seg = sizes
    return (
        (0, 0, comp),
        (comp, OLDC, fresh),
        (comp + fresh, CMEM, mem),
        (comp + fresh + mem, CMEM + MEM, seg),
    )


def in_order(full, own, other, tier, sizes):
    for row, pos, rows in key_pieces(sizes):
        mine = pl.multiple_of(pos + tier * rows, rows)
        theirs = pl.multiple_of(pos + (1 - tier) * rows, rows)
        full[pl.ds(mine, rows)] = own[0, row : row + rows]
        full[pl.ds(theirs, rows)] = other[0, row : row + rows]


def forward_kernel(
    sizes, at, q, k_own, k_other, v_own, v_other, table, cb, pb, att, probs, kf, vf
):
    b = pl.program_id(0)
    tier = at[0]
    comp_fill, mem_fill, seg_len = at[1 + 3 * b], at[2 + 3 * b], at[3 + 3 * b]
    rows = q.shape[1]
    keys = kf.shape[0]
    in_order(kf, k_own, k_other, tier, sizes)
    in_order(vf, v_own, v_other, tier, sizes)
    query = q[0].astype(F32)
    content_q = (query + cb[0]).astype(BF16)
    position_q = (query + pb[0]).astype(BF16)
    scale = 1.0 / math.sqrt(q.shape[2])
    relative = dot(position_q, table[...], ((1,), (1,)))
    relative = pltpu.roll(relative, keys - rows + 1, 1, stride=1, stride_axis=0)
    scores = (dot(content_q, kf[...], ((1,), (1,))) + relative) * scale
    start = CMEM + MEM
    j = lax.broadcasted_iota(jnp.int32, (1, keys), 1)
    lowest = jnp.where(
        j < CMEM, CMEM - comp_fill, jnp.where(j < start, start - mem_fill, start)
    )
    beyond = jnp.where(j < start, start, start + seg_len)
    open_col = (j >= lowest) & (j < beyond)
    bias = jnp.where(open_col, 0.0, NEG)
    i = lax.broadcasted_iota(jnp.int32, (rows, keys), 0) + tier * rows
    jj = lax.broadcasted_iota(jnp.int32, (rows, keys), 1) - start
    masked = jnp.where(jj <= i, scores + bias, NEG)
    peak = jnp.max(masked, axis=-1, keepdims=True)
    e = jnp.exp(masked - peak)
    total = jnp.sum(e, axis=-1, keepdims=True)
    p = (e * (1.0 / total)).astype(BF16)
    probs[0, 0] = p
    att[0] = dot(p, vf[...], ((1,), (0,))).astype(BF16)


def attend(at, q, kv, kv_other, table, cb, pb, sizes):
    batch, rows, width = q.shape
    heads = cb.shape[0]
    hd = width // heads
    keys_local = kv.shape[1]
    keys = 2 * keys_local

    def col(off):
        return pl.BlockSpec((1, keys_local, hd), lambda b, h, s: (b, 0, h + off))

    return pl.pallas_call(
        functools.partial(forward_kernel, sizes),
        grid_spec=pltpu.PrefetchScalarGridSpec(
            num_scalar_prefetch=1,
            grid=(batch, heads),
            in_specs=[
                pl.BlockSpec((1, rows, hd), lambda b, h, s: (b, 0, h)),
                col(0),
                col(0),
                col(heads),
                col(heads),
                pl.BlockSpec((keys, hd), lambda b, h, s: (0, h)),
                pl.BlockSpec((1, 1, hd), lambda b, h, s: (h, 0, 0)),
                pl.BlockSpec((1, 1, hd), lambda b, h, s: (h, 0, 0)),
            ],
            out_specs=[
                pl.BlockSpec((1, rows, hd), lambda b, h, s: (b, 0, h)),
                pl.BlockSpec((1, 1, rows, keys), lambda b, h, s: (b, h, 0, 0)),
            ],
            scratch_shapes=[pltpu.VMEM((keys, hd), BF16), pltpu.VMEM((keys, hd), BF16)],
        ),
        out_shape=[
            jax.ShapeDtypeStruct((batch, rows, width), BF16),
            jax.ShapeDtypeStruct((batch, heads, rows, keys), BF16),
        ],
        compiler_params=pltpu.CompilerParams(vmem_limit_bytes=48 << 20),
        cost_estimate=pl.CostEstimate(
            flops=batch * heads * 6 * rows * keys * hd,
            bytes_accessed=batch * heads * rows * keys * 2,
            transcendentals=batch * heads * rows * keys,
        ),
        name="attend",
    )(at, q, kv, kv_other, kv, kv_other, table, cb[:, None], pb[:, None])


def backward_kernel(
    sizes,
    at,
    probs,
    gatt,
    q,
    k_own,
    k_other,
    v_own,
    v_other,
    table,
    cb,
    pb,
    gq,
    keep,
    send,
    gtable,
    gbias,
    kf,
    vf,
    gk,
):
    first = pl.program_id(1) == 0
    tier = at[0]
    rows = q.shape[1]
    in_order(kf, k_own, k_other, tier, sizes)
    in_order(vf, v_own, v_other, tier, sizes)
    query = q[0].astype(F32)
    content_q = (query + cb[0]).astype(BF16)
    position_q = (query + pb[0]).astype(BF16)
    scale = 1.0 / math.sqrt(q.shape[2])
    ga = gatt[0]
    p_low = probs[0, 0]
    p = p_low.astype(F32)
    gp = dot(ga, vf[...], ((1,), (1,)))
    row_dot = jnp.sum(p * gp, axis=-1, keepdims=True)
    ds = (p * (gp - row_dot)).astype(BF16)

    def hand_out(which, value):
        gk[...] = value.astype(BF16)
        for row, pos, size in key_pieces(sizes):
            mine = pl.multiple_of(pos + tier * size, size)
            theirs = pl.multiple_of(pos + (1 - tier) * size, size)
            keep[which, 0, row : row + size] = gk[pl.ds(mine, size)]
            send[which, 0, row : row + size] = gk[pl.ds(theirs, size)]

    hand_out(0, dot(ds, content_q, ((0,), (0,))) * scale)
    hand_out(1, dot(p_low, ga, ((0,), (0,))))
    g_content = dot(ds, kf[...], ((1,), (0,))) * scale
    r = lax.broadcasted_iota(jnp.int32, (rows, rows), 0)
    c = lax.broadcasted_iota(jnp.int32, (rows, rows), 1)
    flip = jnp.where(r + c == rows - 1, 1.0, 0.0).astype(BF16)
    ds_flip = dot(flip, ds, ((1,), (0,)))
    skewed = pltpu.roll(ds_flip, 0, 1, stride=1, stride_axis=0).astype(BF16)
    position_flip = dot(flip, position_q, ((1,), (0,))).astype(BF16)
    g_table = dot(skewed, position_flip, ((0,), (0,))) * scale
    g_flip = dot(skewed, table[...], ((1,), (0,))) * scale
    high = g_flip.astype(BF16)
    low = (g_flip - high.astype(F32)).astype(BF16)
    g_position = dot(flip, high, ((1,), (0,))) + dot(flip, low, ((1,), (0,)))
    gq[0] = (g_content + g_position).astype(BF16)
    sums = jnp.concatenate(
        [
            jnp.sum(g_content, axis=0, keepdims=True),
            jnp.sum(g_position, axis=0, keepdims=True),
            jnp.zeros((6, g_content.shape[1]), F32),
        ],
        axis=0,
    )

    @pl.when(first)
    def _():
        gtable[...] = g_table
        gbias[0] = sums

    @pl.when(jnp.logical_not(first))
    def _():
        gtable[...] += g_table
        gbias[0] += sums


def attend_back(at, probs, gatt, q, kv, kv_other, table, cb, pb, sizes):
    batch, rows, width = q.shape
    heads = cb.shape[0]
    hd = width // heads
    keys_local = kv.shape[1]
    keys = 2 * keys_local

    def col(off):
        return pl.BlockSpec((1, keys_local, hd), lambda h, b, s: (b, 0, h + off))

    def row_block():
        return pl.BlockSpec((1, rows, hd), lambda h, b, s: (b, 0, h))

    def half():
        return pl.BlockSpec((2, 1, keys_local, hd), lambda h, b, s: (0, b, 0, h))

    return pl.pallas_call(
        functools.partial(backward_kernel, sizes),
        grid_spec=pltpu.PrefetchScalarGridSpec(
            num_scalar_prefetch=1,
            grid=(heads, batch),
            in_specs=[
                pl.BlockSpec((1, 1, rows, keys), lambda h, b, s: (b, h, 0, 0)),
                row_block(),
                row_block(),
                col(0),
                col(0),
                col(heads),
                col(heads),
                pl.BlockSpec((keys, hd), lambda h, b, s: (0, h)),
                pl.BlockSpec((1, 1, hd), lambda h, b, s: (h, 0, 0)),
                pl.BlockSpec((1, 1, hd), lambda h, b, s: (h, 0, 0)),
            ],
            out_specs=[
                row_block(),
                half(),
                half(),
                pl.BlockSpec((keys, hd), lambda h, b, s: (0, h)),
                pl.BlockSpec((1, 8, hd), lambda h, b, s: (h, 0, 0)),
            ],
            scratch_shapes=[pltpu.VMEM((keys, hd), BF16)] * 3,
        ),
        out_shape=[
            jax.ShapeDtypeStruct((batch, rows, width), BF16),
            jax.ShapeDtypeStruct((2, batch, keys_local, width), BF16),
            jax.ShapeDtypeStruct((2, batch, keys_local, width), BF16),
            jax.ShapeDtypeStruct((keys, width), F32),
            jax.ShapeDtypeStruct((heads, 8, hd), F32),
        ],
        compiler_params=pltpu.CompilerParams(vmem_limit_bytes=48 << 20),
        cost_estimate=pl.CostEstimate(
            flops=batch * heads * 14 * rows * keys * hd,
            bytes_accessed=batch * heads * rows * keys * 2,
            transcendentals=0,
        ),
        name="attend_back",
    )(at, probs, gatt, q, kv, kv_other, kv, kv_other, table, cb[:, None], pb[:, None])


def distance_rows(first, count):
    half = D // 2
    freq = np.exp(np.arange(half) * (-2.0 * math.log(10000.0) / D))
    turned = (first - np.arange(count))[:, None] * freq[None, :]
    return np.concatenate([np.sin(turned), np.cos(turned)], axis=1).astype(
        ml_dtypes.bfloat16
    )


def standardize(rows):
    mean = jnp.mean(rows, axis=-1, keepdims=True)
    centred = rows - mean
    var = jnp.mean(centred * centred, axis=-1, keepdims=True)
    r = lax.rsqrt(var + EPS)
    return centred * r, r


def norm_back(grad, xhat, r, gain):
    g = grad * gain
    return r * (
        g
        - jnp.mean(g, axis=-1, keepdims=True)
        - xhat * jnp.mean(g * xhat, axis=-1, keepdims=True)
    )


def col_sum(x):
    return jnp.sum(x, axis=tuple(range(x.ndim - 1)))


def ein(spec, a, b):
    return jnp.einsum(spec, a, b, preferred_element_type=F32)


def shards(
    segment_input,
    memory,
    compressed,
    evicted,
    cotangent,
    seg_lengths,
    memory_fills,
    compressed_fills,
    conv_weight,
    conv_bias,
    norm1_gain,
    norm1_bias,
    query_weight,
    key_weight,
    value_weight,
    position_weight,
    content_bias,
    position_bias,
    out_weight,
    norm2_gain,
    norm2_bias,
    up_weight,
    up_bias,
    down_weight,
    down_bias,
):
    tier = lax.axis_index("tier")
    head = lax.axis_index("head")
    batch, seg, _ = segment_input.shape
    mem = memory.shape[1]
    comp = compressed.shape[1]
    fresh = evicted.shape[1] // KW
    sizes = (comp, fresh, mem, seg)
    width = query_weight.shape[1]
    wide = conv_weight.shape[2]
    hidden = up_weight.shape[1]
    keys = 2 * (comp + fresh + mem + seg)

    attn_w = gather_rows(
        jnp.concatenate([key_weight, value_weight, query_weight, position_weight], 1)
    )
    conv_w = gather_rows(jnp.concatenate([conv_weight[k] for k in range(KW)], 1))
    out_t = head_gather(out_weight.T)
    ffn_w = gather_rows(jnp.concatenate([out_t, up_weight, down_weight.T], 1))
    kv_w = attn_w[:, : 2 * width]
    q_w = attn_w[:, 2 * width : 3 * width]
    pos_w = attn_w[:, 3 * width :]
    full_width = out_t.shape[1]
    out_wt = ffn_w[:, :full_width]
    up_w = ffn_w[:, full_width : full_width + hidden]
    down_wt = ffn_w[:, full_width + hidden :]

    grouped = evicted.reshape(batch, fresh, KW, D)
    fresh_part = conv_bias
    for k in range(KW):
        fresh_part = fresh_part + ein(
            "bgc,cd->bgd", grouped[:, :, k], conv_w[:, k * wide : (k + 1) * wide]
        )
    fresh_rows = head_gather(fresh_part.astype(BF16))
    context = jnp.concatenate([compressed, fresh_rows, memory, segment_input], axis=1)
    xhat, r_one = standardize(context.astype(F32))
    normed = (xhat * norm1_gain + norm1_bias).astype(BF16)
    split = comp + fresh + mem
    kv = ein("brd,de->bre", normed, kv_w).astype(BF16)
    own_normed = normed[:, split:]
    q = ein("brd,de->bre", own_normed, q_w).astype(BF16)
    kv_other = swap(kv, "tier")
    far = keys - 1
    steps = jnp.asarray(distance_rows(far, keys + seg))
    steps = lax.dynamic_slice_in_dim(steps, (1 - tier) * seg, keys, 0)
    table = ein("nf,fe->ne", steps, pos_w).astype(BF16)
    at = jnp.concatenate(
        [
            tier[None].astype(jnp.int32),
            jnp.stack([compressed_fills, memory_fills, seg_lengths], 1).reshape(-1),
        ]
    )
    att, probs = attend(at, q, kv, kv_other, table, content_bias, position_bias, sizes)
    att_full = head_gather(att)
    branch = ein("bre,de->brd", att_full, out_wt)
    hidden_one = segment_input.astype(F32) + branch

    xhat_two, r_two = standardize(hidden_one)
    normed_two = (xhat_two * norm2_gain + norm2_bias).astype(BF16)
    pre = ein("brd,df->brf", normed_two, up_w) + up_bias
    activated_f, gate_pull = jax.vjp(
        lambda v: jax.nn.gelu(v, approximate=True), pre
    )
    activated = activated_f.astype(BF16)
    live = (tier * seg + jnp.arange(seg))[None, :] < seg_lengths[:, None]
    grad_out = jnp.where(live[:, :, None], cotangent, jnp.zeros((), BF16))
    grad_act = ein("brd,df->brf", grad_out, down_wt)
    grad_pre = gate_pull(grad_act)[0].astype(BF16)
    grad_two = head_sum(ein("brf,df->brd", grad_pre, up_w).astype(BF16))
    ffn = head_sum(ein("brf,df->brd", activated, down_wt).astype(BF16))
    output = (hidden_one + ffn + down_bias).astype(BF16)

    grad_up = ein("brd,brf->df", normed_two, grad_pre).astype(BF16)
    grad_down_t = ein("brd,brf->df", grad_out, activated).astype(BF16)
    grad_hidden = grad_out.astype(F32) + norm_back(grad_two, xhat_two, r_two, norm2_gain)
    grad_branch = grad_hidden.astype(BF16)
    grad_out_t = ein("brd,bre->de", grad_branch, att).astype(BF16)
    mid_sums = small_sum(
        [
            col_sum(grad_two * xhat_two),
            col_sum(grad_two),
            col_sum(grad_pre.astype(F32)),
            col_sum(grad_out.astype(F32)),
        ]
    )
    grad_up_s = reduce_rows(grad_up)
    grad_down_s = reduce_rows(grad_down_t).T
    grad_out_s = reduce_rows(grad_out_t).T

    own_cols = lax.dynamic_slice_in_dim(out_wt, head * width, width, 1)
    gatt = ein("brd,de->bre", grad_branch, own_cols).astype(BF16)
    gq, keep, send, gtable, gbias = attend_back(
        at, probs, gatt, q, kv, kv_other, table, content_bias, position_bias, sizes
    )
    gkv = (keep.astype(F32) + swap(send, "tier").astype(F32)).astype(BF16)
    gk, gv = gkv[0], gkv[1]
    grad_k = ein("brd,bre->de", normed, gk).astype(BF16)
    grad_v = ein("brd,bre->de", normed, gv).astype(BF16)
    grad_q = ein("brd,bre->de", own_normed, gq).astype(BF16)
    grad_pos = ein("nf,ne->fe", steps, gtable.astype(BF16)).astype(BF16)

    grad_n = ein("bre,de->brd", gk, kv_w[:, :width]) + ein(
        "bre,de->brd", gv, kv_w[:, width:]
    )
    grad_q_rows = ein("bre,de->brd", gq, q_w)
    low = comp + fresh
    part = jnp.concatenate(
        [grad_n[:, :low], grad_n[:, split:] + grad_q_rows], axis=1
    ).astype(BF16)
    grad_mem = grad_n[:, low:split]
    mem_sums = jnp.stack([col_sum(grad_mem * xhat[:, low:split]), col_sum(grad_mem)])
    grad_rows = head_sum(part)
    xhat_kept = jnp.concatenate([xhat[:, :low], xhat[:, split:]], axis=1)
    r_kept = jnp.concatenate([r_one[:, :low], r_one[:, split:]], axis=1)
    grad_context = norm_back(grad_rows, xhat_kept, r_kept, norm1_gain)
    grad_comp = grad_context[:, :comp]
    grad_in = grad_hidden + grad_context[:, low:]
    fresh_own = lax.dynamic_slice_in_dim(
        grad_context[:, comp:low], head * wide, wide, 2
    ).astype(BF16)
    grad_conv = jnp.concatenate(
        [ein("bgc,bgd->cd", grouped[:, :, k], fresh_own) for k in range(KW)], axis=1
    ).astype(BF16)
    if lax.axis_size("head") == 2:
        mem_sums = mem_sums + swap(mem_sums, "head")
    else:
        mem_sums = lax.psum(mem_sums, "head")
    end_sums = small_sum(
        [
            col_sum(fresh_own.astype(F32)),
            col_sum(grad_rows * xhat_kept) + mem_sums[0],
            col_sum(grad_rows) + mem_sums[1],
            gbias[:, 0],
            gbias[:, 1],
        ]
    )
    grad_conv_s = reduce_rows(grad_conv)
    grad_conv_s = jnp.stack(
        [grad_conv_s[:, k * wide : (k + 1) * wide] for k in range(KW)]
    )
    return (
        output,
        grad_in,
        grad_comp,
        grad_conv_s,
        end_sums[0],
        end_sums[1],
        end_sums[2],
        reduce_rows(grad_q),
        reduce_rows(grad_k),
        reduce_rows(grad_v),
        reduce_rows(grad_pos),
        end_sums[3],
        end_sums[4],
        grad_out_s,
        mid_sums[0],
        mid_sums[1],
        grad_up_s,
        mid_sums[2],
        grad_down_s,
        mid_sums[3],
    )


def solution(mesh):
    rows = P("dp", "tier", None)
    by_row = P(("dp", "tier"), "head")
    by_col = P("head", ("dp", "tier"))
    conv = P(None, ("dp", "tier"), "head")
    heads = P("head", None)
    placed = (
        (rows,) * 5
        + (P("dp"),) * 3
        + (conv, P("head"), P(), P())
        + (by_row,) * 4
        + (heads, heads, by_col, P(), P(), by_row, P("head"), by_col, P())
    )
    results = (
        (rows,) * 3
        + (conv, P("head"), P(), P())
        + (by_row,) * 4
        + (heads, heads, by_col, P(), P(), by_row, P("head"), by_col, P())
    )
    return jax.shard_map(
        shards, mesh=mesh, in_specs=placed, out_specs=results, check_vma=False
    )
```

```python
import functools
import math

import jax
import jax.numpy as jnp
import ml_dtypes
import numpy as np
from jax import lax
from jax.experimental import pallas as pl
from jax.experimental.pallas import tpu as pltpu
from jax.sharding import PartitionSpec as P

D = 1024
MEM = 512
CMEM = 512
KW = 3
OLDC = 384
EPS = 1e-05
NEG = -1e30
F32 = jnp.float32
BF16 = jnp.bfloat16


def swap(x, axis, step=1):
    n = lax.axis_size(axis)
    return lax.ppermute(x, axis, [(i, i ^ step) for i in range(n)])


def after(x, *others):
    return lax.optimization_barrier((x, *others))[0]


def z_exchange(x):
    n = lax.axis_size("dp")
    groups = [[z * 2 + y for z in range(n // 2)] for y in range(2)]
    return lax.all_to_all(x, "dp", 0, 0, axis_index_groups=groups, tiled=True)


def head_gather(x):
    if lax.axis_size("head") == 2:
        other = swap(x, "head")
        first = lax.axis_index("head") == 0
        return jnp.concatenate(
            [jnp.where(first, x, other), jnp.where(first, other, x)], axis=-1
        )
    return lax.all_gather(x, "head", axis=x.ndim - 1, tiled=True)


def place_kernel(at_ref, b0, b1, b2, b3, out, sems):
    y, t = at_ref[0], at_ref[1]
    copies = []
    for k, block in enumerate((b0, b1, b2, b3)):
        yy = 1 - y if k % 2 else y
        tt = 1 - t if k // 2 else t
        copies.append(pltpu.make_async_copy(block, out.at[:, yy, tt], sems.at[k]))
    for copy in copies:
        copy.start()
    for copy in copies:
        copy.wait()


def gather_z(x):
    zn = lax.axis_size("dp") // 2
    return z_exchange(jnp.broadcast_to(x[None], (zn,) + x.shape))


def gather_yt(over_z):
    other = swap(over_z, "dp")
    return [over_z, other, swap(over_z, "tier"), swap(other, "tier")]


def place(blocks):
    zn, rows, cols = blocks[0].shape
    shape = (zn, 2, 2, rows, cols)
    at = jnp.stack([lax.axis_index("dp") % 2, lax.axis_index("tier")])
    out = pl.pallas_call(
        place_kernel,
        grid_spec=pltpu.PrefetchScalarGridSpec(
            num_scalar_prefetch=1,
            grid=(1,),
            in_specs=[pl.BlockSpec(memory_space=pl.ANY)] * 4,
            out_specs=pl.BlockSpec(shape, lambda i, s: (0, 0, 0, 0, 0)),
            scratch_shapes=[pltpu.SemaphoreType.DMA((4,))],
        ),
        out_shape=jax.ShapeDtypeStruct(shape, blocks[0].dtype),
        compiler_params=pltpu.CompilerParams(vmem_limit_bytes=60 << 20),
        cost_estimate=cost(3),
        name="place",
    )(at.astype(jnp.int32), *blocks)
    return out.reshape(zn * 4 * rows, cols)


def small_sum(parts):
    flat = jnp.concatenate([p.reshape(-1) for p in parts])
    pad = -flat.shape[0] % 1024
    flat = jnp.pad(flat, (0, pad)).reshape(-1, 128)
    n = lax.axis_size("dp")
    if n & (n - 1):
        flat = lax.psum(flat, ("dp", "tier"))
    else:
        flat = flat + swap(flat, "tier")
        step = 1
        while step < n:
            flat = flat + swap(flat, "dp", step)
            step *= 2
    flat = flat.reshape(-1)
    out, at = [], 0
    for p in parts:
        out.append(flat[at : at + p.size].reshape(p.shape))
        at += p.size
    return out


def dot(a, b, contract):
    return lax.dot_general(a, b, (contract, ((), ())), preferred_element_type=F32)


NN = ((1,), (0,))
NT = ((1,), (1,))
TN = ((0,), (0,))


def params(mib=60):
    return pltpu.CompilerParams(vmem_limit_bytes=mib << 20)


def cost(us):
    return pl.CostEstimate(
        flops=int(us * 1.15e9), bytes_accessed=1024, transcendentals=0
    )


def whole(shape):
    return pl.BlockSpec(shape, lambda *i: (0,) * len(shape))


def stream(b, rows, cols=D):
    return pl.BlockSpec((1, rows, cols), lambda *i: (b, 0, 0))


def key_pieces(sizes):
    comp, fresh, mem, seg = sizes
    return (
        (0, 0, comp),
        (comp, OLDC, fresh),
        (comp + fresh, CMEM, mem),
        (comp + fresh + mem, CMEM + MEM, seg),
    )


def in_order(full, own, other, tier, sizes):
    for row, pos, rows in key_pieces(sizes):
        mine = pl.multiple_of(pos + tier * rows, rows)
        theirs = pl.multiple_of(pos + (1 - tier) * rows, rows)
        full[pl.ds(mine, rows)] = own[0, row : row + rows]
        full[pl.ds(theirs, rows)] = other[0, row : row + rows]


def project_kernel(comp, fresh, mem, seg, w, normed, kv, q):
    at = 0
    for piece in (comp, fresh, mem, seg):
        rows = piece.shape[1]
        normed[0, at : at + rows] = piece[0]
        at += rows
    width = q.shape[2]
    kv[0] = dot(normed[0], w[:, : 2 * width], NN).astype(BF16)
    first = at - seg.shape[1]
    q[0] = dot(normed[0, first:], w[:, 2 * width : 3 * width], NN).astype(BF16)


def project(comp, fresh, mem, seg, w):
    batch = comp.shape[0]
    width = w.shape[1] // 4
    pieces = (comp, fresh, mem, seg)
    rows = sum(p.shape[1] for p in pieces)

    def block(n, cols=D):
        return pl.BlockSpec((1, n, cols), lambda b: (b, 0, 0))

    shapes = ((rows, D), (rows, 2 * width), (seg.shape[1], width))
    return pl.pallas_call(
        project_kernel,
        grid=(batch,),
        in_specs=[block(p.shape[1]) for p in pieces] + [whole(w.shape)],
        out_specs=[block(*shape) for shape in shapes],
        out_shape=[jax.ShapeDtypeStruct((batch,) + shape, BF16) for shape in shapes],
        compiler_params=params(),
        cost_estimate=cost(50),
        name="project",
    )(*pieces, w)


def forward_kernel(
    b, sizes, at, q, k_own, k_other, v_own, v_other, table, cb, pb, att, probs, kf, vf
):
    tier = at[0]
    comp_fill, mem_fill, seg_len = at[2 + 3 * b], at[3 + 3 * b], at[4 + 3 * b]
    rows = q.shape[1]
    keys = kf.shape[0]
    in_order(kf, k_own, k_other, tier, sizes)
    in_order(vf, v_own, v_other, tier, sizes)
    query = q[0].astype(F32)
    content_q = (query + cb[0]).astype(BF16)
    position_q = (query + pb[0]).astype(BF16)
    scale = 1.0 / math.sqrt(q.shape[2])
    relative = dot(position_q, table[...], NT)
    relative = pltpu.roll(relative, keys - rows + 1, 1, stride=1, stride_axis=0)
    scores = (dot(content_q, kf[...], NT) + relative) * scale
    start = CMEM + MEM
    j = lax.broadcasted_iota(jnp.int32, (1, keys), 1)
    lowest = jnp.where(
        j < CMEM, CMEM - comp_fill, jnp.where(j < start, start - mem_fill, start)
    )
    beyond = jnp.where(j < start, start, start + seg_len)
    open_col = (j >= lowest) & (j < beyond)
    bias = jnp.where(open_col, 0.0, NEG)
    i = lax.broadcasted_iota(jnp.int32, (rows, keys), 0) + tier * rows
    jj = lax.broadcasted_iota(jnp.int32, (rows, keys), 1) - start
    masked = jnp.where(jj <= i, scores + bias, NEG)
    peak = jnp.max(masked, axis=-1, keepdims=True)
    e = jnp.exp(masked - peak)
    total = jnp.sum(e, axis=-1, keepdims=True)
    p = (e * (1.0 / total)).astype(BF16)
    probs[0] = p
    att[...] = dot(p, vf[...], NN).astype(BF16)


def attend(b, at, q, kv, kv_other, table, cb, pb, sizes):
    _, rows, width = q.shape
    heads = cb.shape[0]
    hd = width // heads
    keys_local = kv.shape[1]
    keys = 2 * keys_local

    def col(off):
        return pl.BlockSpec((1, keys_local, hd), lambda h, s: (b, 0, h + off))

    def bias():
        return pl.BlockSpec((1, 1, hd), lambda h, s: (h, 0, 0))

    return pl.pallas_call(
        functools.partial(forward_kernel, b, sizes),
        grid_spec=pltpu.PrefetchScalarGridSpec(
            num_scalar_prefetch=1,
            grid=(heads,),
            in_specs=[
                pl.BlockSpec((1, rows, hd), lambda h, s: (b, 0, h)),
                col(0),
                col(0),
                col(heads),
                col(heads),
                pl.BlockSpec((keys, hd), lambda h, s: (0, h)),
                bias(),
                bias(),
            ],
            out_specs=[
                pl.BlockSpec((rows, hd), lambda h, s: (0, h)),
                pl.BlockSpec((1, rows, keys), lambda h, s: (h, 0, 0)),
            ],
            scratch_shapes=[pltpu.VMEM((keys, hd), BF16), pltpu.VMEM((keys, hd), BF16)],
        ),
        out_shape=[
            jax.ShapeDtypeStruct((rows, width), BF16),
            jax.ShapeDtypeStruct((heads, rows, keys), BF16),
        ],
        compiler_params=params(),
        cost_estimate=cost(20),
        name="attend",
    )(at, q, kv, kv_other, kv, kv_other, table, cb[:, None], pb[:, None])


def standardize(rows):
    mean = jnp.mean(rows, axis=-1, keepdims=True)
    centred = rows - mean
    var = jnp.mean(centred * centred, axis=-1, keepdims=True)
    r = lax.rsqrt(var + EPS)
    return centred * r, r


def norm_back(grad, xhat, r, gain):
    g = grad * gain
    return r * (
        g
        - jnp.mean(g, axis=-1, keepdims=True)
        - xhat * jnp.mean(g * xhat, axis=-1, keepdims=True)
    )


def row_sums(values, width):
    sums = [jnp.sum(v, axis=0, keepdims=True) for v in values]
    return jnp.concatenate(sums + [jnp.zeros((8 - len(sums), width), F32)], axis=0)


def ffn_kernel(batch, parts, full, at, *refs):
    count = batch * parts
    atts = refs[:count]
    x, cot, gain, shift, up_b, w = refs[count : count + 6]
    outs = refs[count + 6 :]
    kept_out, (sums_up, sums_out) = outs[:5], outs[5:7]
    twos, ffns = outs[7 : 7 + batch], outs[7 + batch : 7 + 2 * batch]
    kept, (wv, w_sem, sem) = outs[7 + 2 * batch : -3], outs[-3:]
    hidden, n2, go, act, gpre = kept
    hid = act.shape[1]
    hb = min(512, hid)
    steps = hid // hb
    tier, head = at[0], at[1]
    rows = x.shape[1]

    def fetch(k, first, cols):
        part = slice(first, first + cols)
        return pltpu.make_async_copy(w.at[:, part], wv.at[:, part], w_sem.at[k])

    copies = [fetch(0, 0, full), fetch(1, full, hid), fetch(2, full + hid, hid)]
    for copy in copies:
        copy.start()
    going = []

    def give(k, cols):
        copy = pltpu.make_async_copy(
            kept[k].at[:, cols], kept_out[k].at[:, cols], sem.at[len(going)]
        )
        copy.start()
        going.append(copy)

    every = slice(0, D)
    total = None
    for b in range(batch):
        row = lax.broadcasted_iota(jnp.int32, (rows, 1), 0) + tier * rows
        masked = jnp.where(row < at[4 + 3 * b], cot[b].astype(F32), 0.0)
        go[b * rows : (b + 1) * rows] = masked.astype(BF16)
        sums = row_sums([masked], D)
        total = sums if total is None else total + sums
    sums_out[...] = total
    give(2, every)
    copies[0].wait()
    if parts == 2:
        first = head == 0
        att = jnp.concatenate(
            [
                jnp.concatenate(
                    [
                        jnp.where(first, atts[2 * b][...], atts[2 * b + 1][...]),
                        jnp.where(first, atts[2 * b + 1][...], atts[2 * b][...]),
                    ],
                    axis=1,
                )
                for b in range(batch)
            ],
            axis=0,
        )
    else:
        att = jnp.concatenate([a[...] for a in atts], axis=0)
    h = x[...].reshape(batch * rows, D).astype(F32) + dot(att, wv[:, :full], NT)
    hidden[...] = h
    give(0, every)
    xhat, _ = standardize(h)
    n2[...] = (xhat * gain[...] + shift[...]).astype(BF16)
    give(1, every)
    copies[1].wait()
    copies[2].wait()
    c = math.sqrt(2.0 / math.pi)
    ck = c * 0.044715
    for j in range(steps):
        cols = slice(j * hb, (j + 1) * hb)
        up = wv[:, full + j * hb : full + (j + 1) * hb]
        down = wv[:, full + hid + j * hb : full + hid + (j + 1) * hb]
        pre = dot(n2[...], up, NN) + up_b[:, cols]
        g_act = dot(go[...], down, NN)
        sq = pre * pre
        half = 0.5 + 0.5 * jnp.tanh(pre * (c + ck * sq))
        a = pre * half
        slope = half + a * (1.0 - half) * (2 * c + 6 * ck * sq)
        g = (g_act * slope).astype(BF16)
        act[:, cols] = a.astype(BF16)
        gpre[:, cols] = g
        sums_up[:, cols] = row_sums([g.astype(F32)], hb)
        give(3, cols)
        give(4, cols)
    for outs_of, k, first in ((twos, 4, full), (ffns, 3, full + hid)):
        product = dot(kept[k][...], wv[:, first : first + hid], NT).astype(BF16)
        for b in range(batch):
            outs_of[b][...] = product[b * rows : (b + 1) * rows]
    for copy in going:
        copy.wait()


def feed_forward(at, atts, x, cot, w_ffn, full, gain, shift, up_b):
    batch, rows, _ = x.shape
    hidden_n = (w_ffn.shape[1] - full) // 2
    steps = hidden_n // min(512, hidden_n)
    every = batch * rows
    anywhere = pl.BlockSpec(memory_space=pl.ANY)
    kept = [(D, F32), (D, BF16), (D, BF16), (hidden_n, BF16), (hidden_n, BF16)]
    return pl.pallas_call(
        functools.partial(ffn_kernel, batch, len(atts) // batch, full),
        grid_spec=pltpu.PrefetchScalarGridSpec(
            num_scalar_prefetch=1,
            grid=(1,),
            in_specs=[whole(a.shape) for a in atts]
            + [whole(x.shape)] * 2
            + [whole((1, D)), whole((1, D)), whole((1, hidden_n)), anywhere],
            out_specs=[anywhere] * 5
            + [whole((8, hidden_n)), whole((8, D))]
            + [whole((rows, D))] * (2 * batch),
            scratch_shapes=[pltpu.VMEM((every, n), dtype) for n, dtype in kept]
            + [
                pltpu.VMEM(w_ffn.shape, BF16),
                pltpu.SemaphoreType.DMA((3,)),
                pltpu.SemaphoreType.DMA((3 + 2 * steps,)),
            ],
        ),
        out_shape=[jax.ShapeDtypeStruct((every, n), dtype) for n, dtype in kept]
        + [jax.ShapeDtypeStruct((8, hidden_n), F32), jax.ShapeDtypeStruct((8, D), F32)]
        + [jax.ShapeDtypeStruct((rows, D), BF16)] * (2 * batch),
        compiler_params=params(),
        cost_estimate=cost(50),
        name="feed_forward",
    )(at, *atts, x, cot, gain[None], shift[None], up_b[None], w_ffn)


def backward_kernel(sizes, parts, chained, at, *refs):
    twos, refs = refs[:parts], refs[parts:]
    hidden, go, gain, w = refs[:4]
    (probs, q, k_own, k_other, v_own, v_other, table, cb, pb) = refs[4:13]
    refs = refs[13:]
    if chained:
        before, refs = refs[0], refs[1:]
    ghid, gbr, sums, gq, keep, send, gtable, gbias, kf, vf, gk, gatt = refs
    tier = at[0]
    step = pl.program_id(0)
    rows, hd = q.shape[1], q.shape[2]

    @pl.when(step == 0)
    def _():
        grad = summed(twos, slice(None))
        xhat, r = standardize(hidden[...])
        g = go[...].astype(F32) + norm_back(grad, xhat, r, gain[...])
        ghid[...] = g
        low = g.astype(BF16)
        gbr[...] = low
        out = dot(low, w[...], NN).astype(BF16)
        for k in range(gatt.shape[0]):
            gatt[k] = out[:, k * hd : (k + 1) * hd]
        sums[...] = row_sums([grad * xhat, grad], D)

    @pl.when(step > 0)
    def _():
        in_order(kf, k_own, k_other, tier, sizes)
        in_order(vf, v_own, v_other, tier, sizes)
        query = q[0].astype(F32)
        content_q = (query + cb[0]).astype(BF16)
        position_q = (query + pb[0]).astype(BF16)
        scale = 1.0 / math.sqrt(hd)
        ga = gatt[step - 1]
        p_low = probs[0]
        p = p_low.astype(F32)
        gp = dot(ga, vf[...], NT)
        row_dot = jnp.sum(p * gp, axis=-1, keepdims=True)
        ds = (p * (gp - row_dot)).astype(BF16)

        def hand_out(which, value):
            gk[...] = value.astype(BF16)
            for row, pos, size in key_pieces(sizes):
                mine = pl.multiple_of(pos + tier * size, size)
                theirs = pl.multiple_of(pos + (1 - tier) * size, size)
                keep[which, row : row + size] = gk[pl.ds(mine, size)]
                send[which, row : row + size] = gk[pl.ds(theirs, size)]

        hand_out(0, dot(ds, content_q, TN) * scale)
        hand_out(1, dot(p_low, ga, TN))
        g_content = dot(ds, kf[...], NN) * scale
        r = lax.broadcasted_iota(jnp.int32, (rows, rows), 0)
        c = lax.broadcasted_iota(jnp.int32, (rows, rows), 1)
        flip = jnp.where(r + c == rows - 1, 1.0, 0.0).astype(BF16)
        ds_flip = dot(flip, ds, NN)
        skewed = pltpu.roll(ds_flip, 0, 1, stride=1, stride_axis=0).astype(BF16)
        position_flip = dot(flip, position_q, NN).astype(BF16)
        g_table = dot(position_flip, skewed, TN) * scale
        g_flip = dot(skewed, table[...], NN) * scale
        high = g_flip.astype(BF16)
        low = (g_flip - high.astype(F32)).astype(BF16)
        g_position = dot(flip, high, NN) + dot(flip, low, NN)
        gq[...] = (g_content + g_position).astype(BF16)
        gbias[0] = row_sums([g_content, g_position], hd)
        if chained:
            g_table = g_table + before[...]
        gtable[...] = g_table


def attend_back(
    b, at, twos, hidden, go, gain, w, probs, q, kv, kv_other, table, cb, pb, sizes, before
):
    _, rows, width = q.shape
    heads = cb.shape[0]
    hd = width // heads
    keys_local = kv.shape[1]
    keys = 2 * keys_local
    chained = before is not None

    def of(h):
        return jnp.maximum(h - 1, 0)

    def col(off):
        return pl.BlockSpec((1, keys_local, hd), lambda h, s: (b, 0, of(h) + off))

    def half():
        return pl.BlockSpec((2, keys_local, hd), lambda h, s: (0, 0, of(h)))

    def bias():
        return pl.BlockSpec((1, 1, hd), lambda h, s: (of(h), 0, 0))

    def turned():
        return pl.BlockSpec((hd, keys), lambda h, s: (of(h), 0))

    def own_rows():
        return pl.BlockSpec((rows, D), lambda h, s: (b, 0))

    args = [at, *twos, hidden, go, gain[None], w]
    args += [probs, q, kv, kv_other, kv, kv_other, table]
    args += [cb[:, None], pb[:, None]]
    return pl.pallas_call(
        functools.partial(backward_kernel, sizes, len(twos), chained),
        grid_spec=pltpu.PrefetchScalarGridSpec(
            num_scalar_prefetch=1,
            grid=(1 + heads,),
            in_specs=[whole((rows, D)) for _ in twos]
            + [
                own_rows(),
                own_rows(),
                whole((1, D)),
                pl.BlockSpec((D, width), lambda h, s: (0, s[1])),
                pl.BlockSpec((1, rows, keys), lambda h, s: (of(h), 0, 0)),
                pl.BlockSpec((1, rows, hd), lambda h, s: (b, 0, of(h))),
                col(0),
                col(0),
                col(heads),
                col(heads),
                pl.BlockSpec((keys, hd), lambda h, s: (0, of(h))),
                bias(),
                bias(),
            ]
            + ([turned()] if chained else []),
            out_specs=[
                whole((rows, D)),
                whole((rows, D)),
                whole((8, D)),
                pl.BlockSpec((rows, hd), lambda h, s: (0, of(h))),
                half(),
                half(),
                turned(),
                pl.BlockSpec((1, 8, hd), lambda h, s: (of(h), 0, 0)),
            ],
            scratch_shapes=[pltpu.VMEM((keys, hd), BF16)] * 3
            + [pltpu.VMEM((heads, rows, hd), BF16)],
        ),
        out_shape=[
            jax.ShapeDtypeStruct((rows, D), F32),
            jax.ShapeDtypeStruct((rows, D), BF16),
            jax.ShapeDtypeStruct((8, D), F32),
            jax.ShapeDtypeStruct((rows, width), BF16),
            jax.ShapeDtypeStruct((2, keys_local, width), BF16),
            jax.ShapeDtypeStruct((2, keys_local, width), BF16),
            jax.ShapeDtypeStruct((width, keys), F32),
            jax.ShapeDtypeStruct((heads, 8, hd), F32),
        ],
        compiler_params=params(),
        cost_estimate=cost(50),
        name="attend_back",
    )(*args, *([before] if chained else []))


def rows_kernel(sizes, keep, got, gq, normed_mem, w, gkv, part, fpart, sums, both):
    comp, fresh, mem, seg = sizes
    width = gq.shape[1]

    @pl.when(pl.program_id(0) == 0)
    def _():
        for k in range(2):
            total = keep[k].astype(F32) + got[k].astype(F32)
            both[:, k * width : (k + 1) * width] = total.astype(BF16)
        gkv[...] = both[...]

    low = comp + fresh
    split = low + mem
    grad = dot(both[...], w[:, : 2 * width], NT)
    part[:comp] = grad[:comp].astype(BF16)
    fpart[...] = grad[comp:low].astype(BF16)
    part[comp:] = (
        grad[split:] + dot(gq[...], w[:, 2 * width : 3 * width], NT)
    ).astype(BF16)
    g_mem = grad[low:split]
    sums[...] = row_sums([g_mem * normed_mem[0].astype(F32), g_mem], g_mem.shape[1])


def rows_back(b, keep, got, gq, normed_mem, w, sizes):
    width = gq.shape[1]
    local = keep.shape[1]
    comp, fresh, mem, seg = sizes
    kept = comp + seg
    db = 256
    return pl.pallas_call(
        functools.partial(rows_kernel, sizes),
        grid=(D // db,),
        in_specs=[
            whole((2, local, width)),
            whole((2, local, width)),
            whole((seg, width)),
            pl.BlockSpec((1, mem, db), lambda j: (b, 0, j)),
            pl.BlockSpec((db, 4 * width), lambda j: (j, 0)),
        ],
        out_specs=[
            whole((local, 2 * width)),
            pl.BlockSpec((kept, db), lambda j: (0, j)),
            pl.BlockSpec((fresh, db), lambda j: (0, j)),
            pl.BlockSpec((8, db), lambda j: (0, j)),
        ],
        out_shape=[
            jax.ShapeDtypeStruct((local, 2 * width), BF16),
            jax.ShapeDtypeStruct((kept, D), BF16),
            jax.ShapeDtypeStruct((fresh, D), BF16),
            jax.ShapeDtypeStruct((8, D), F32),
        ],
        scratch_shapes=[pltpu.VMEM((local, 2 * width), BF16)],
        compiler_params=params(),
        cost_estimate=cost(3),
        name="rows_back",
    )(keep, got, gq, normed_mem, w)


def summed(refs, part):
    total = refs[0][part].astype(F32)
    for other in refs[1:]:
        total = total + other[part].astype(F32)
    return total


def context_kernel(sizes, parts, chained, *refs):
    grads = refs[:parts]
    comp, seg, ghid, gain = refs[parts : parts + 4]
    gcomp, gin, sums = refs[parts + 4 + (2 if chained else 0) :]
    rows = comp.shape[1]
    total = None
    for raw, part in ((comp, slice(0, rows)), (seg, slice(rows, None))):
        grad = summed(grads, part)
        xhat, r = standardize(raw[0].astype(F32))
        g = norm_back(grad, xhat, r, gain[...])
        part_sums = row_sums([grad * xhat, grad], D)
        if total is None:
            gcomp[0] = g
            total = part_sums
        else:
            gin[0] = ghid[...] + g
            total = total + part_sums
    sums[...] = total


def context_back(b, grads, comp, seg, ghid, gain, before, sizes):
    batch = comp.shape[0]
    kept = grads[0].shape[0]
    chained = before is not None
    n_comp, _, _, n_seg = sizes
    first = len(grads) + 4
    return pl.pallas_call(
        functools.partial(context_kernel, sizes, len(grads), chained),
        grid=(1,),
        in_specs=[whole((kept, D)) for _ in grads]
        + [stream(b, n_comp), stream(b, n_seg), whole((n_seg, D)), whole((1, D))]
        + ([pl.BlockSpec(memory_space=pl.ANY)] * 2 if chained else []),
        out_specs=[stream(b, n_comp), stream(b, n_seg), whole((8, D))],
        out_shape=[
            jax.ShapeDtypeStruct((batch, n_comp, D), F32),
            jax.ShapeDtypeStruct((batch, n_seg, D), F32),
            jax.ShapeDtypeStruct((8, D), F32),
        ],
        input_output_aliases={first: 0, first + 1: 1} if chained else {},
        compiler_params=params(),
        cost_estimate=cost(3),
        name="context_back",
    )(*grads, comp, seg, ghid, gain[None], *(before if chained else ()))


def fresh_kernel(batch, *refs):
    count = len(refs) - 4
    raw, gain, gfresh, sums = refs[count:]
    per = count // batch
    total = None
    for b in range(batch):
        grad = summed(refs[b * per : (b + 1) * per], slice(None))
        xhat, r = standardize(raw[b].astype(F32))
        rows = xhat.shape[0]
        g = norm_back(grad, xhat, r, gain[...])
        gfresh[b * rows : (b + 1) * rows] = g.astype(BF16)
        part_sums = row_sums([grad * xhat, grad, g.astype(BF16).astype(F32)], D)
        total = part_sums if total is None else total + part_sums
    sums[...] = total


def fresh_back(grads, raw, gain):
    batch, rows, _ = raw.shape
    flat = [g for pair in grads for g in pair]
    return pl.pallas_call(
        functools.partial(fresh_kernel, batch),
        grid=(1,),
        in_specs=[whole((rows, D)) for _ in flat] + [whole(raw.shape), whole((1, D))],
        out_specs=[whole((batch * rows, D)), whole((8, D))],
        out_shape=[
            jax.ShapeDtypeStruct((batch * rows, D), BF16),
            jax.ShapeDtypeStruct((8, D), F32),
        ],
        compiler_params=params(),
        cost_estimate=cost(2),
        name="fresh_back",
    )(*flat, raw, gain[None])


def table_kernel(at, steps, w, out):
    out[...] = dot(steps[...], w[...], NN).astype(BF16)


def position_table(at, steps, w, seg, keys, col, width):
    return pl.pallas_call(
        table_kernel,
        grid_spec=pltpu.PrefetchScalarGridSpec(
            num_scalar_prefetch=1,
            grid=(keys // seg,),
            in_specs=[
                pl.BlockSpec((seg, D), lambda i, s: (1 - s[0] + i, 0)),
                pl.BlockSpec((D, width), lambda i, s: (0, col)),
            ],
            out_specs=pl.BlockSpec((seg, width), lambda i, s: (i, 0)),
        ),
        out_shape=jax.ShapeDtypeStruct((keys, width), BF16),
        compiler_params=params(),
        cost_estimate=cost(20),
        name="position_table",
    )(at, steps, w)


def grad_ffn_kernel(steps, n2, gpre, go, act, out):
    j = pl.program_id(0)

    @pl.when(j < steps)
    def _():
        out[...] = dot(n2[...], gpre[...], TN).astype(BF16)

    @pl.when(j >= steps)
    def _():
        out[...] = dot(go[...], act[...], TN).astype(BF16)


def grad_ffn(n2, gpre, go, act):
    rows, hidden = act.shape
    hb = min(512, hidden)
    steps = hidden // hb

    def block(first):
        return pl.BlockSpec(
            (rows, hb), lambda j: (0, jnp.clip(j - first, 0, steps - 1))
        )

    return pl.pallas_call(
        functools.partial(grad_ffn_kernel, steps),
        grid=(2 * steps,),
        in_specs=[whole((rows, D)), block(0), whole((rows, D)), block(steps)],
        out_specs=pl.BlockSpec((D, hb), lambda j: (0, j)),
        out_shape=jax.ShapeDtypeStruct((D, 2 * hidden), BF16),
        compiler_params=params(),
        cost_estimate=cost(30),
        name="grad_ffn",
    )(n2, gpre, go, act)


def fill(y, ys):
    rows = ys[0].shape[0]
    for k, part in enumerate(ys):
        y[k * rows : (k + 1) * rows] = part[...]


def grad_kv_kernel(batch, x, *refs):
    ys, (_, out, y) = refs[:batch], refs[batch:]
    fill(y, ys)
    out[...] = dot(x[...], y[...], TN).astype(BF16)


def grad_kv(x, ys, grads, col, width):
    every = x.shape[0]
    return pl.pallas_call(
        functools.partial(grad_kv_kernel, len(ys)),
        grid=(2,),
        in_specs=[whole(x.shape)]
        + [pl.BlockSpec((y.shape[0], width), lambda j: (0, j)) for y in ys]
        + [pl.BlockSpec(memory_space=pl.ANY)],
        out_specs=pl.BlockSpec((D, width), lambda j: (0, col + j)),
        scratch_shapes=[pltpu.VMEM((every, width), BF16)],
        out_shape=jax.ShapeDtypeStruct(grads.shape, BF16),
        input_output_aliases={1 + len(ys): 0},
        compiler_params=params(),
        cost_estimate=cost(8),
        name="grad_kv",
    )(x, *ys, grads)


def grad_rest_kernel(batch, at, normed, *refs):
    gq, gbr, att = (refs[k * batch : (k + 1) * batch] for k in range(3))
    steps, gtable, out, x, y = refs[3 * batch :]
    j = pl.program_id(0)
    tier = at[0]

    @pl.when(j == 0)
    def _():
        fill(x, [normed.at[k] for k in range(batch)])
        fill(y, gq)

    @pl.when(j == 1)
    def _():
        fill(x, gbr)
        fill(y, att)

    @pl.when(j < 2)
    def _():
        out[...] = dot(x[...], y[...], TN).astype(BF16)

    @pl.when(j == 2)
    def _():
        keys = gtable.shape[1]
        seg = steps.shape[0] - keys
        first = pl.multiple_of((1 - tier) * seg, seg)
        turned = dot(gtable[...].astype(BF16), steps[pl.ds(first, keys)], NN)
        out[...] = turned.astype(BF16).T


def grad_rest(at, normed, gq, gbr, att, steps, gtable, cols):
    seg, width = gq[0].shape
    batch, local, _ = normed.shape
    return pl.pallas_call(
        functools.partial(grad_rest_kernel, batch),
        grid_spec=pltpu.PrefetchScalarGridSpec(
            num_scalar_prefetch=1,
            grid=(3,),
            in_specs=[
                pl.BlockSpec((batch, seg, D), lambda j, s: (0, local // seg - 1, 0))
            ]
            + [whole((seg, width))] * batch
            + [whole((seg, D))] * batch
            + [whole((seg, width))] * batch
            + [whole(steps.shape), whole(gtable.shape)],
            out_specs=pl.BlockSpec((D, width), lambda j, s: (0, j)),
            scratch_shapes=[
                pltpu.VMEM((batch * seg, D), BF16),
                pltpu.VMEM((batch * seg, width), BF16),
            ],
        ),
        out_shape=jax.ShapeDtypeStruct((D, cols), BF16),
        compiler_params=params(),
        cost_estimate=cost(8),
        name="grad_rest",
    )(at, normed, *gq, *gbr, *att, steps, gtable)


def grad_conv_kernel(at, taps, fresh, _, out):
    out[...] = dot(taps[...], fresh[...], TN).astype(BF16)


def grad_conv(at, grouped, fresh, grads, col, wide):
    count = grouped.shape[0]
    return pl.pallas_call(
        grad_conv_kernel,
        grid_spec=pltpu.PrefetchScalarGridSpec(
            num_scalar_prefetch=1,
            grid=(KW,),
            in_specs=[
                pl.BlockSpec((count, D), lambda j, s: (0, j)),
                pl.BlockSpec((count, wide), lambda j, s: (0, s[1])),
                pl.BlockSpec(memory_space=pl.ANY),
            ],
            out_specs=pl.BlockSpec((D, wide), lambda j, s: (0, col + j)),
        ),
        out_shape=jax.ShapeDtypeStruct(grads.shape, BF16),
        input_output_aliases={3: 0},
        compiler_params=params(),
        cost_estimate=cost(4),
        name="grad_conv",
    )(at, grouped, fresh, grads)


def conv_kernel(taps, w, bias, out):
    k = pl.program_id(0)
    part = dot(taps[...], w[...], NN)

    @pl.when(k == 0)
    def _():
        out[...] = part + bias[...]

    @pl.when(k > 0)
    def _():
        out[...] += part


def compress(grouped, w, bias):
    count = grouped.shape[0]
    wide = bias.shape[0]
    return pl.pallas_call(
        conv_kernel,
        grid=(KW,),
        in_specs=[
            pl.BlockSpec((count, D), lambda j: (0, j)),
            pl.BlockSpec((D, wide), lambda j: (0, j)),
            whole((1, wide)),
        ],
        out_specs=whole((count, wide)),
        out_shape=jax.ShapeDtypeStruct((count, wide), F32),
        compiler_params=params(),
        cost_estimate=cost(3),
        name="compress",
    )(grouped, w, bias[None])


def distance_rows(first, count):
    half = D // 2
    freq = np.exp(np.arange(half) * (-2.0 * math.log(10000.0) / D))
    turned = (first - np.arange(count))[:, None] * freq[None, :]
    return np.concatenate([np.sin(turned), np.cos(turned)], axis=1).astype(
        ml_dtypes.bfloat16
    )


def col_sum(x):
    return jnp.sum(x, axis=tuple(range(x.ndim - 1)))


def ein(spec, a, b):
    return jnp.einsum(spec, a, b, preferred_element_type=F32)


def norm_rows(rows, gain, shift):
    return (standardize(rows.astype(F32))[0] * gain + shift).astype(BF16)


def shards(
    segment_input,
    memory,
    compressed,
    evicted,
    cotangent,
    seg_lengths,
    memory_fills,
    compressed_fills,
    conv_weight,
    conv_bias,
    norm1_gain,
    norm1_bias,
    query_weight,
    key_weight,
    value_weight,
    position_weight,
    content_bias,
    position_bias,
    out_weight,
    norm2_gain,
    norm2_bias,
    up_weight,
    up_bias,
    down_weight,
    down_bias,
):
    tier = lax.axis_index("tier")
    head = lax.axis_index("head")
    heads_n = lax.axis_size("head")
    batch, seg, _ = segment_input.shape
    mem = memory.shape[1]
    comp = compressed.shape[1]
    fresh = evicted.shape[1] // KW
    sizes = (comp, fresh, mem, seg)
    width = query_weight.shape[1]
    wide = conv_weight.shape[2]
    hidden = up_weight.shape[1]
    keys = 2 * (comp + fresh + mem + seg)
    streams = range(batch)
    at = jnp.concatenate(
        [
            jnp.stack([tier, head]).astype(jnp.int32),
            jnp.stack([compressed_fills, memory_fills, seg_lengths], 1).reshape(-1),
        ]
    )


    conv_z = gather_z(jnp.concatenate([conv_weight[k] for k in range(KW)], 1))
    out_t = head_gather(out_weight.T)
    full = out_t.shape[1]
    attn_pack = jnp.concatenate(
        [key_weight, value_weight, query_weight, position_weight], 1
    )
    ffn_pack = jnp.concatenate([out_t, up_weight, down_weight.T], 1)
    attn_z = gather_z(after(attn_pack, conv_z, out_t))
    ffn_w = lax.all_gather(
        after(ffn_pack, conv_z), ("dp", "tier"), axis=0, tiled=True
    )
    conv_blocks = gather_yt(conv_z)
    conv_blocks[0] = after(conv_blocks[0], out_t)
    conv_w = place(conv_blocks)

    n_comp = norm_rows(compressed, norm1_gain, norm1_bias)
    n_mem = norm_rows(memory, norm1_gain, norm1_bias)
    n_seg = norm_rows(segment_input, norm1_gain, norm1_bias)
    grouped = evicted.reshape(batch * fresh, KW * D)
    fresh_part = compress(grouped, conv_w, conv_bias).astype(BF16)
    fresh_rows = head_gather(fresh_part.reshape(batch, fresh, wide))
    n_fresh = norm_rows(fresh_rows, norm1_gain, norm1_bias)
    attn_blocks = gather_yt(attn_z)
    attn_blocks[0] = after(attn_blocks[0], fresh_part)
    attn_w = place(attn_blocks)

    normed, kv, q = project(n_comp, n_fresh, n_mem, n_seg, attn_w)
    kv_other = swap(kv, "tier")
    steps = jnp.asarray(distance_rows(keys - 1, keys + seg))
    table = position_table(at, steps, after(attn_w, kv), seg, keys, 3, width)
    atts, probs, others = [], [], []
    for b in streams:
        q_b = after(q, *(others[-2:-1] + atts[-1:])) if b else after(q, table)
        att, p = attend(
            b, at, q_b, kv, kv_other, table, content_bias, position_bias, sizes
        )
        atts.append(att)
        probs.append(p)
        if heads_n == 2:
            others.append(swap(att, "head"))
        else:
            others.append(lax.all_gather(att, "head", axis=1, tiled=True))

    def over_head(x):
        if heads_n == 2:
            return [x, swap(x, "head")]
        return [lax.psum(x, "head")]

    if heads_n == 2:
        pairs = [v for pair in zip(atts, others) for v in pair]
    else:
        pairs = others
    hid, n2, go, act, gpre, up_sums, out_sums, *halves = feed_forward(
        at,
        pairs,
        segment_input,
        cotangent,
        ffn_w,
        full,
        norm2_gain,
        norm2_bias,
        up_bias,
    )
    twos = [over_head(halves[0])]
    g_ffn = grad_ffn(n2, gpre, go, act)
    g_ffn_s = lax.psum_scatter(
        g_ffn, ("dp", "tier"), scatter_dimension=0, tiled=True
    ).astype(F32)

    ghids, gbrs, gqs, keeps, gots = [], [], [], [], []
    gkvs, parts, fparts, downs = [], [], [], []
    bias_sums, mem_sums, mid_rows = 0, 0, 0
    gtable = None
    last = g_ffn

    def rows_of(b, *others):
        gq = after(gqs[b], *others)
        gkv, part, fpart, sums = rows_back(
            b, keeps[b], gots[b], gq, n_mem, attn_w, sizes
        )
        gkvs.append(gkv)
        if b == batch - 1:
            fparts.append(over_head(fpart))
            parts.append(over_head(after(part, fparts[-1][-1])))
        else:
            parts.append(over_head(part))
            fparts.append(over_head(fpart))
        return sums[:2], part

    for b in streams:
        if b > 1:
            sums, last = rows_of(b - 2, last)
            mem_sums = mem_sums + sums
        if b < batch - 1:
            twos.append(over_head(after(halves[b + 1], twos[b][-1])))
        ghid, gbr, sums, gq, keep, send, gtable, gbias = attend_back(
            b,
            at,
            twos[b],
            hid,
            after(go, last),
            norm2_gain,
            ffn_w,
            probs[b],
            q,
            kv,
            kv_other,
            table,
            content_bias,
            position_bias,
            sizes,
            gtable,
        )
        last = gq
        ghids.append(ghid)
        gbrs.append(gbr)
        gqs.append(gq)
        keeps.append(keep)
        gots.append(swap(send, "tier"))
        if 0 < b:
            downs.append(over_head(after(halves[batch + b - 1], gq)))
        mid_rows = mid_rows + sums
        bias_sums = bias_sums + gbias
    cols = 5 * width + KW * wide
    gq_0 = after(gqs[0], last, parts[0][-1])
    grads = grad_rest(
        at, normed, [gq_0] + gqs[1:], gbrs, atts, steps, gtable, cols
    )
    last = grads
    for b in range(max(batch - 2, 0), batch):
        sums, last = rows_of(b, last)
        mem_sums = mem_sums + sums
    mem_sums = sum(over_head(mem_sums))
    grads = grad_kv(
        after(normed, mem_sums).reshape(-1, D), gkvs, grads, 3, width
    )
    fresh_grad, fresh_sums = fresh_back(
        fparts, after(fresh_rows, g_ffn_s), norm1_gain
    )
    grads = grad_conv(at, grouped, fresh_grad, grads, 5 * width // wide, wide)
    grads_s = lax.psum_scatter(
        grads, ("dp", "tier"), scatter_dimension=0, tiled=True
    ).astype(F32)
    g_q, g_out, g_pos, g_k, g_v = (
        grads_s[:, k * width : (k + 1) * width] for k in range(5)
    )
    g_conv = jnp.stack(
        [
            grads_s[:, 5 * width + k * wide : 5 * width + (k + 1) * wide]
            for k in range(KW)
        ]
    )
    downs.append(over_head(after(halves[-1], parts[-1][-1])))
    row_totals = fresh_sums[:2]
    gcomp = gin = None
    for b in streams:
        gcomp, gin, sums = context_back(
            b,
            parts[b],
            compressed,
            segment_input,
            after(ghids[b], grads if b == 0 else gin),
            norm1_gain,
            (gcomp, gin) if b else None,
            sizes,
        )
        row_totals = row_totals + sums[:2]
    grad_comp, grad_in = gcomp, gin

    outs = []
    for b in streams:
        out = hid[b * seg : (b + 1) * seg] + down_bias
        for x in downs[b]:
            out = out + x.astype(F32)
        outs.append(out.astype(BF16))
    output = jnp.stack(outs)
    mem_gain = (mem_sums[0] - norm1_bias * mem_sums[1]) / norm1_gain
    fresh_sum = lax.dynamic_slice_in_dim(fresh_sums[2], head * wide, wide, 0)
    sums = small_sum(
        [
            mid_rows[0],
            mid_rows[1],
            up_sums[0],
            out_sums[0],
            fresh_sum,
            row_totals[0] + mem_gain,
            row_totals[1] + mem_sums[1],
            bias_sums[:, 0],
            bias_sums[:, 1],
        ]
    )
    return (
        output,
        grad_in,
        grad_comp,
        g_conv,
        sums[4],
        sums[5],
        sums[6],
        g_q,
        g_k,
        g_v,
        g_pos,
        sums[7],
        sums[8],
        g_out.T,
        sums[0],
        sums[1],
        g_ffn_s[:, :hidden],
        sums[2],
        g_ffn_s[:, hidden:].T,
        sums[3],
    )


def solution(mesh):
    rows = P("dp", "tier", None)
    by_row = P(("dp", "tier"), "head")
    by_col = P("head", ("dp", "tier"))
    conv = P(None, ("dp", "tier"), "head")
    heads = P("head", None)
    placed = (
        (rows,) * 5
        + (P("dp"),) * 3
        + (conv, P("head"), P(), P())
        + (by_row,) * 4
        + (heads, heads, by_col, P(), P(), by_row, P("head"), by_col, P())
    )
    results = (
        (rows,) * 3
        + (conv, P("head"), P(), P())
        + (by_row,) * 4
        + (heads, heads, by_col, P(), P(), by_row, P("head"), by_col, P())
    )
    return jax.shard_map(
        shards, mesh=mesh, in_specs=placed, out_specs=results, check_vma=False
    )
```

```python
import functools
import math

import jax
import jax.numpy as jnp
import ml_dtypes
import numpy as np
from jax import lax
from jax.experimental import pallas as pl
from jax.experimental.pallas import tpu as pltpu
from jax.sharding import PartitionSpec as P

D = 1024
MEM = 512
CMEM = 512
KW = 3
OLDC = 384
EPS = 1e-05
NEG = -1e30
F32 = jnp.float32
BF16 = jnp.bfloat16


def swap(x, axis, step=1):
    n = lax.axis_size(axis)
    return lax.ppermute(x, axis, [(i, i ^ step) for i in range(n)])


def after(x, *others):
    return lax.optimization_barrier((x, *others))[0]


def z_exchange(x):
    n = lax.axis_size("dp")
    groups = [[z * 2 + y for z in range(n // 2)] for y in range(2)]
    return lax.all_to_all(x, "dp", 0, 0, axis_index_groups=groups, tiled=True)


def head_gather(x):
    if lax.axis_size("head") == 2:
        other = swap(x, "head")
        first = lax.axis_index("head") == 0
        return jnp.concatenate(
            [jnp.where(first, x, other), jnp.where(first, other, x)], axis=-1
        )
    return lax.all_gather(x, "head", axis=x.ndim - 1, tiled=True)


def place_kernel(at_ref, b0, b1, b2, b3, out, sems):
    y, t = at_ref[0], at_ref[1]
    copies = []
    for k, block in enumerate((b0, b1, b2, b3)):
        yy = 1 - y if k % 2 else y
        tt = 1 - t if k // 2 else t
        copies.append(pltpu.make_async_copy(block, out.at[:, yy, tt], sems.at[k]))
    for copy in copies:
        copy.start()
    for copy in copies:
        copy.wait()


def gather_z(x):
    zn = lax.axis_size("dp") // 2
    return z_exchange(jnp.broadcast_to(x[None], (zn,) + x.shape))


def gather_yt(over_z):
    other = swap(over_z, "dp")
    return [over_z, other, swap(over_z, "tier"), swap(other, "tier")]


def place(blocks):
    zn, rows, cols = blocks[0].shape
    shape = (zn, 2, 2, rows, cols)
    at = jnp.stack([lax.axis_index("dp") % 2, lax.axis_index("tier")])
    out = pl.pallas_call(
        place_kernel,
        grid_spec=pltpu.PrefetchScalarGridSpec(
            num_scalar_prefetch=1,
            grid=(1,),
            in_specs=[pl.BlockSpec(memory_space=pl.ANY)] * 4,
            out_specs=pl.BlockSpec(shape, lambda i, s: (0, 0, 0, 0, 0)),
            scratch_shapes=[pltpu.SemaphoreType.DMA((4,))],
        ),
        out_shape=jax.ShapeDtypeStruct(shape, blocks[0].dtype),
        compiler_params=pltpu.CompilerParams(vmem_limit_bytes=60 << 20),
        cost_estimate=cost(3),
        name="place",
    )(at.astype(jnp.int32), *blocks)
    return out.reshape(zn * 4 * rows, cols)


def add_low(a, b):
    return (a.astype(F32) + b.astype(F32)).astype(BF16)


def halve(keep, got):
    zn = lax.axis_size("dp") // 2
    y = lax.axis_index("dp") % 2
    shape = (zn, 2, keep.shape[0] // (2 * zn), keep.shape[1])
    keep, got = keep.reshape(shape), got.reshape(shape)

    def pick(k):
        a, b = (lax.dynamic_index_in_dim(v, k, 1, keepdims=False) for v in (keep, got))
        return add_low(a, b)

    return pick(y), pick(1 - y)


def small_sum(parts):
    flat = jnp.concatenate([p.reshape(-1) for p in parts])
    pad = -flat.shape[0] % 1024
    flat = jnp.pad(flat, (0, pad)).reshape(-1, 128)
    n = lax.axis_size("dp")
    if n & (n - 1):
        flat = lax.psum(flat, ("dp", "tier"))
    else:
        flat = flat + swap(flat, "tier")
        step = 1
        while step < n:
            flat = flat + swap(flat, "dp", step)
            step *= 2
    flat = flat.reshape(-1)
    out, at = [], 0
    for p in parts:
        out.append(flat[at : at + p.size].reshape(p.shape))
        at += p.size
    return out


def dot(a, b, contract):
    return lax.dot_general(a, b, (contract, ((), ())), preferred_element_type=F32)


NN = ((1,), (0,))
NT = ((1,), (1,))
TN = ((0,), (0,))


def params(mib=60):
    return pltpu.CompilerParams(vmem_limit_bytes=mib << 20)


def cost(us):
    return pl.CostEstimate(
        flops=int(us * 1.15e9), bytes_accessed=1024, transcendentals=0
    )


def whole(shape):
    return pl.BlockSpec(shape, lambda *i: (0,) * len(shape))


def stream(b, rows, cols=D):
    return pl.BlockSpec((1, rows, cols), lambda *i: (b, 0, 0))


def key_pieces(sizes):
    comp, fresh, mem, seg = sizes
    return (
        (0, 0, comp),
        (comp, OLDC, fresh),
        (comp + fresh, CMEM, mem),
        (comp + fresh + mem, CMEM + MEM, seg),
    )


def in_order(full, own, other, tier, sizes):
    for row, pos, rows in key_pieces(sizes):
        mine = pl.multiple_of(pos + tier * rows, rows)
        theirs = pl.multiple_of(pos + (1 - tier) * rows, rows)
        full[pl.ds(mine, rows)] = own[0, row : row + rows]
        full[pl.ds(theirs, rows)] = other[0, row : row + rows]


def project_kernel(comp, fresh, mem, seg, w, normed, kv, q):
    at = 0
    for piece in (comp, fresh, mem, seg):
        rows = piece.shape[1]
        normed[0, at : at + rows] = piece[0]
        at += rows
    width = q.shape[2]
    kv[0] = dot(normed[0], w[:, : 2 * width], NN).astype(BF16)
    first = at - seg.shape[1]
    q[0] = dot(normed[0, first:], w[:, 2 * width : 3 * width], NN).astype(BF16)


def project(comp, fresh, mem, seg, w):
    batch = comp.shape[0]
    width = w.shape[1] // 4
    pieces = (comp, fresh, mem, seg)
    rows = sum(p.shape[1] for p in pieces)

    def block(n, cols=D):
        return pl.BlockSpec((1, n, cols), lambda b: (b, 0, 0))

    shapes = ((rows, D), (rows, 2 * width), (seg.shape[1], width))
    return pl.pallas_call(
        project_kernel,
        grid=(batch,),
        in_specs=[block(p.shape[1]) for p in pieces] + [whole(w.shape)],
        out_specs=[block(*shape) for shape in shapes],
        out_shape=[jax.ShapeDtypeStruct((batch,) + shape, BF16) for shape in shapes],
        compiler_params=params(),
        cost_estimate=cost(50),
        name="project",
    )(*pieces, w)


def forward_kernel(
    b, sizes, at, q, k_own, k_other, v_own, v_other, table, cb, pb, att, probs, kf, vf
):
    tier = at[0]
    comp_fill, mem_fill, seg_len = at[2 + 3 * b], at[3 + 3 * b], at[4 + 3 * b]
    rows = q.shape[1]
    keys = kf.shape[0]
    in_order(kf, k_own, k_other, tier, sizes)
    in_order(vf, v_own, v_other, tier, sizes)
    query = q[0].astype(F32)
    content_q = (query + cb[0]).astype(BF16)
    position_q = (query + pb[0]).astype(BF16)
    scale = 1.0 / math.sqrt(q.shape[2])
    relative = dot(position_q, table[...], NT)
    relative = pltpu.roll(relative, keys - rows + 1, 1, stride=1, stride_axis=0)
    scores = (dot(content_q, kf[...], NT) + relative) * scale
    start = CMEM + MEM
    j = lax.broadcasted_iota(jnp.int32, (1, keys), 1)
    lowest = jnp.where(
        j < CMEM, CMEM - comp_fill, jnp.where(j < start, start - mem_fill, start)
    )
    beyond = jnp.where(j < start, start, start + seg_len)
    open_col = (j >= lowest) & (j < beyond)
    bias = jnp.where(open_col, 0.0, NEG)
    i = lax.broadcasted_iota(jnp.int32, (rows, keys), 0) + tier * rows
    jj = lax.broadcasted_iota(jnp.int32, (rows, keys), 1) - start
    masked = jnp.where(jj <= i, scores + bias, NEG)
    peak = jnp.max(masked, axis=-1, keepdims=True)
    e = jnp.exp(masked - peak)
    total = jnp.sum(e, axis=-1, keepdims=True)
    p = (e * (1.0 / total)).astype(BF16)
    probs[0] = p
    att[...] = dot(p, vf[...], NN).astype(BF16)


def attend(b, at, q, kv, kv_other, table, cb, pb, sizes):
    _, rows, width = q.shape
    heads = cb.shape[0]
    hd = width // heads
    keys_local = kv.shape[1]
    keys = 2 * keys_local

    def col(off):
        return pl.BlockSpec((1, keys_local, hd), lambda h, s: (b, 0, h + off))

    def bias():
        return pl.BlockSpec((1, 1, hd), lambda h, s: (h, 0, 0))

    return pl.pallas_call(
        functools.partial(forward_kernel, b, sizes),
        grid_spec=pltpu.PrefetchScalarGridSpec(
            num_scalar_prefetch=1,
            grid=(heads,),
            in_specs=[
                pl.BlockSpec((1, rows, hd), lambda h, s: (b, 0, h)),
                col(0),
                col(0),
                col(heads),
                col(heads),
                pl.BlockSpec((keys, hd), lambda h, s: (0, h)),
                bias(),
                bias(),
            ],
            out_specs=[
                pl.BlockSpec((rows, hd), lambda h, s: (0, h)),
                pl.BlockSpec((1, rows, keys), lambda h, s: (h, 0, 0)),
            ],
            scratch_shapes=[pltpu.VMEM((keys, hd), BF16), pltpu.VMEM((keys, hd), BF16)],
        ),
        out_shape=[
            jax.ShapeDtypeStruct((rows, width), BF16),
            jax.ShapeDtypeStruct((heads, rows, keys), BF16),
        ],
        compiler_params=params(),
        cost_estimate=cost(20),
        name="attend",
    )(at, q, kv, kv_other, kv, kv_other, table, cb[:, None], pb[:, None])


def standardize(rows):
    mean = jnp.mean(rows, axis=-1, keepdims=True)
    centred = rows - mean
    var = jnp.mean(centred * centred, axis=-1, keepdims=True)
    r = lax.rsqrt(var + EPS)
    return centred * r, r


def norm_back(grad, xhat, r, gain):
    g = grad * gain
    return r * (
        g
        - jnp.mean(g, axis=-1, keepdims=True)
        - xhat * jnp.mean(g * xhat, axis=-1, keepdims=True)
    )


def row_sums(values, width):
    sums = [jnp.sum(v, axis=0, keepdims=True) for v in values]
    return jnp.concatenate(sums + [jnp.zeros((8 - len(sums), width), F32)], axis=0)


def ffn_kernel(batch, parts, full, at, *refs):
    count = batch * parts
    atts = refs[:count]
    x, cot, gain, shift, up_b, w = refs[count : count + 6]
    outs = refs[count + 6 :]
    kept_out, (sums_up, sums_out) = outs[:5], outs[5:7]
    twos, ffns = outs[7 : 7 + batch], outs[7 + batch : 7 + 2 * batch]
    kept, (wv, w_sem, sem) = outs[7 + 2 * batch : -3], outs[-3:]
    hidden, n2, go, act, gpre = kept
    hid = act.shape[1]
    hb = min(512, hid)
    steps = hid // hb
    tier, head = at[0], at[1]
    rows = x.shape[1]

    def fetch(k, first, cols):
        part = slice(first, first + cols)
        return pltpu.make_async_copy(w.at[:, part], wv.at[:, part], w_sem.at[k])

    copies = [fetch(0, 0, full), fetch(1, full, hid), fetch(2, full + hid, hid)]
    for copy in copies:
        copy.start()
    going = []

    def give(k, cols):
        copy = pltpu.make_async_copy(
            kept[k].at[:, cols], kept_out[k].at[:, cols], sem.at[len(going)]
        )
        copy.start()
        going.append(copy)

    every = slice(0, D)
    total = None
    for b in range(batch):
        row = lax.broadcasted_iota(jnp.int32, (rows, 1), 0) + tier * rows
        masked = jnp.where(row < at[4 + 3 * b], cot[b].astype(F32), 0.0)
        go[b * rows : (b + 1) * rows] = masked.astype(BF16)
        sums = row_sums([masked], D)
        total = sums if total is None else total + sums
    sums_out[...] = total
    give(2, every)
    copies[0].wait()
    if parts == 2:
        first = head == 0
        att = jnp.concatenate(
            [
                jnp.concatenate(
                    [
                        jnp.where(first, atts[2 * b][...], atts[2 * b + 1][...]),
                        jnp.where(first, atts[2 * b + 1][...], atts[2 * b][...]),
                    ],
                    axis=1,
                )
                for b in range(batch)
            ],
            axis=0,
        )
    else:
        att = jnp.concatenate([a[...] for a in atts], axis=0)
    h = x[...].reshape(batch * rows, D).astype(F32) + dot(att, wv[:, :full], NT)
    hidden[...] = h
    give(0, every)
    xhat, _ = standardize(h)
    n2[...] = (xhat * gain[...] + shift[...]).astype(BF16)
    give(1, every)
    copies[1].wait()
    copies[2].wait()
    c = math.sqrt(2.0 / math.pi)
    ck = c * 0.044715
    for j in range(steps):
        cols = slice(j * hb, (j + 1) * hb)
        up = wv[:, full + j * hb : full + (j + 1) * hb]
        down = wv[:, full + hid + j * hb : full + hid + (j + 1) * hb]
        pre = dot(n2[...], up, NN) + up_b[:, cols]
        g_act = dot(go[...], down, NN)
        sq = pre * pre
        half = 0.5 + 0.5 * jnp.tanh(pre * (c + ck * sq))
        a = pre * half
        slope = half + a * (1.0 - half) * (2 * c + 6 * ck * sq)
        g = (g_act * slope).astype(BF16)
        act[:, cols] = a.astype(BF16)
        gpre[:, cols] = g
        sums_up[:, cols] = row_sums([g.astype(F32)], hb)
        give(3, cols)
        give(4, cols)
    for outs_of, k, first in ((twos, 4, full), (ffns, 3, full + hid)):
        product = dot(kept[k][...], wv[:, first : first + hid], NT).astype(BF16)
        for b in range(batch):
            outs_of[b][...] = product[b * rows : (b + 1) * rows]
    for copy in going:
        copy.wait()


def feed_forward(at, atts, x, cot, w_ffn, full, gain, shift, up_b):
    batch, rows, _ = x.shape
    hidden_n = (w_ffn.shape[1] - full) // 2
    steps = hidden_n // min(512, hidden_n)
    every = batch * rows
    anywhere = pl.BlockSpec(memory_space=pl.ANY)
    kept = [(D, F32), (D, BF16), (D, BF16), (hidden_n, BF16), (hidden_n, BF16)]
    return pl.pallas_call(
        functools.partial(ffn_kernel, batch, len(atts) // batch, full),
        grid_spec=pltpu.PrefetchScalarGridSpec(
            num_scalar_prefetch=1,
            grid=(1,),
            in_specs=[whole(a.shape) for a in atts]
            + [whole(x.shape)] * 2
            + [whole((1, D)), whole((1, D)), whole((1, hidden_n)), anywhere],
            out_specs=[anywhere] * 5
            + [whole((8, hidden_n)), whole((8, D))]
            + [whole((rows, D))] * (2 * batch),
            scratch_shapes=[pltpu.VMEM((every, n), dtype) for n, dtype in kept]
            + [
                pltpu.VMEM(w_ffn.shape, BF16),
                pltpu.SemaphoreType.DMA((3,)),
                pltpu.SemaphoreType.DMA((3 + 2 * steps,)),
            ],
        ),
        out_shape=[jax.ShapeDtypeStruct((every, n), dtype) for n, dtype in kept]
        + [jax.ShapeDtypeStruct((8, hidden_n), F32), jax.ShapeDtypeStruct((8, D), F32)]
        + [jax.ShapeDtypeStruct((rows, D), BF16)] * (2 * batch),
        compiler_params=params(),
        cost_estimate=cost(50),
        name="feed_forward",
    )(at, *atts, x, cot, gain[None], shift[None], up_b[None], w_ffn)


def backward_kernel(sizes, parts, chained, at, *refs):
    twos, refs = refs[:parts], refs[parts:]
    hidden, go, gain, w = refs[:4]
    (probs, q, k_own, k_other, v_own, v_other, table, cb, pb) = refs[4:13]
    refs = refs[13:]
    if chained:
        before, refs = refs[0], refs[1:]
    ghid, gbr, sums, gq, keep, send, gtable, gbias, kf, vf, gk, gatt = refs
    tier = at[0]
    step = pl.program_id(0)
    rows, hd = q.shape[1], q.shape[2]

    @pl.when(step == 0)
    def _():
        grad = summed(twos, slice(None))
        xhat, r = standardize(hidden[...])
        g = go[...].astype(F32) + norm_back(grad, xhat, r, gain[...])
        ghid[...] = g
        low = g.astype(BF16)
        gbr[...] = low
        out = dot(low, w[...], NN).astype(BF16)
        for k in range(gatt.shape[0]):
            gatt[k] = out[:, k * hd : (k + 1) * hd]
        sums[...] = row_sums([grad * xhat, grad], D)

    @pl.when(step > 0)
    def _():
        in_order(kf, k_own, k_other, tier, sizes)
        in_order(vf, v_own, v_other, tier, sizes)
        query = q[0].astype(F32)
        content_q = (query + cb[0]).astype(BF16)
        position_q = (query + pb[0]).astype(BF16)
        scale = 1.0 / math.sqrt(hd)
        ga = gatt[step - 1]
        p_low = probs[0]
        p = p_low.astype(F32)
        gp = dot(ga, vf[...], NT)
        row_dot = jnp.sum(p * gp, axis=-1, keepdims=True)
        ds = (p * (gp - row_dot)).astype(BF16)

        def hand_out(which, value):
            gk[...] = value.astype(BF16)
            for row, pos, size in key_pieces(sizes):
                mine = pl.multiple_of(pos + tier * size, size)
                theirs = pl.multiple_of(pos + (1 - tier) * size, size)
                keep[which, row : row + size] = gk[pl.ds(mine, size)]
                send[which, row : row + size] = gk[pl.ds(theirs, size)]

        hand_out(0, (dot(content_q, ds, TN) * scale).T)
        hand_out(1, dot(ga, p_low, TN).T)
        g_content = dot(ds, kf[...], NN) * scale
        r = lax.broadcasted_iota(jnp.int32, (rows, rows), 0)
        c = lax.broadcasted_iota(jnp.int32, (rows, rows), 1)
        flip = jnp.where(r + c == rows - 1, 1.0, 0.0).astype(BF16)
        ds_flip = dot(flip, ds, NN)
        skewed = pltpu.roll(ds_flip, 0, 1, stride=1, stride_axis=0).astype(BF16)
        position_flip = dot(flip, position_q, NN).astype(BF16)
        g_table = dot(position_flip, skewed, TN) * scale
        g_flip = dot(skewed, table[...], NN) * scale
        high = g_flip.astype(BF16)
        low = (g_flip - high.astype(F32)).astype(BF16)
        g_position = dot(flip, high, NN) + dot(flip, low, NN)
        gq[...] = (g_content + g_position).astype(BF16)
        gbias[0] = row_sums([g_content, g_position], hd)
        if chained:
            g_table = g_table + before[...]
        gtable[...] = g_table


def attend_back(
    b, at, twos, hidden, go, gain, w, probs, q, kv, kv_other, table, cb, pb, sizes, before
):
    _, rows, width = q.shape
    heads = cb.shape[0]
    hd = width // heads
    keys_local = kv.shape[1]
    keys = 2 * keys_local
    chained = before is not None

    def of(h):
        return jnp.maximum(h - 1, 0)

    def col(off):
        return pl.BlockSpec((1, keys_local, hd), lambda h, s: (b, 0, of(h) + off))

    def half():
        return pl.BlockSpec((2, keys_local, hd), lambda h, s: (0, 0, of(h)))

    def bias():
        return pl.BlockSpec((1, 1, hd), lambda h, s: (of(h), 0, 0))

    def turned():
        return pl.BlockSpec((hd, keys), lambda h, s: (of(h), 0))

    def own_rows():
        return pl.BlockSpec((rows, D), lambda h, s: (b, 0))

    args = [at, *twos, hidden, go, gain[None], w]
    args += [probs, q, kv, kv_other, kv, kv_other, table]
    args += [cb[:, None], pb[:, None]]
    return pl.pallas_call(
        functools.partial(backward_kernel, sizes, len(twos), chained),
        grid_spec=pltpu.PrefetchScalarGridSpec(
            num_scalar_prefetch=1,
            grid=(1 + heads,),
            in_specs=[whole((rows, D)) for _ in twos]
            + [
                own_rows(),
                own_rows(),
                whole((1, D)),
                pl.BlockSpec((D, width), lambda h, s: (0, s[1])),
                pl.BlockSpec((1, rows, keys), lambda h, s: (of(h), 0, 0)),
                pl.BlockSpec((1, rows, hd), lambda h, s: (b, 0, of(h))),
                col(0),
                col(0),
                col(heads),
                col(heads),
                pl.BlockSpec((keys, hd), lambda h, s: (0, of(h))),
                bias(),
                bias(),
            ]
            + ([turned()] if chained else []),
            out_specs=[
                whole((rows, D)),
                whole((rows, D)),
                whole((8, D)),
                pl.BlockSpec((rows, hd), lambda h, s: (0, of(h))),
                half(),
                half(),
                turned(),
                pl.BlockSpec((1, 8, hd), lambda h, s: (of(h), 0, 0)),
            ],
            scratch_shapes=[pltpu.VMEM((keys, hd), BF16)] * 3
            + [pltpu.VMEM((heads, rows, hd), BF16)],
        ),
        out_shape=[
            jax.ShapeDtypeStruct((rows, D), F32),
            jax.ShapeDtypeStruct((rows, D), BF16),
            jax.ShapeDtypeStruct((8, D), F32),
            jax.ShapeDtypeStruct((rows, width), BF16),
            jax.ShapeDtypeStruct((2, keys_local, width), BF16),
            jax.ShapeDtypeStruct((2, keys_local, width), BF16),
            jax.ShapeDtypeStruct((width, keys), F32),
            jax.ShapeDtypeStruct((heads, 8, hd), F32),
        ],
        compiler_params=params(),
        cost_estimate=cost(50),
        name="attend_back",
    )(*args, *([before] if chained else []))


def rows_kernel(sizes, keep, got, gq, normed_mem, w, gkv, part, fpart, sums, both):
    comp, fresh, mem, seg = sizes
    width = gq.shape[1]

    @pl.when(pl.program_id(0) == 0)
    def _():
        for k in range(2):
            total = keep[k].astype(F32) + got[k].astype(F32)
            both[:, k * width : (k + 1) * width] = total.astype(BF16)
        gkv[...] = both[...]

    low = comp + fresh
    split = low + mem
    grad = dot(both[...], w[:, : 2 * width], NT)
    part[:comp] = grad[:comp].astype(BF16)
    fpart[...] = grad[comp:low].astype(BF16)
    part[comp:] = (
        grad[split:] + dot(gq[...], w[:, 2 * width : 3 * width], NT)
    ).astype(BF16)
    g_mem = grad[low:split]
    sums[...] = row_sums([g_mem * normed_mem[0].astype(F32), g_mem], g_mem.shape[1])


def rows_back(b, keep, got, gq, normed_mem, w, sizes):
    width = gq.shape[1]
    local = keep.shape[1]
    comp, fresh, mem, seg = sizes
    kept = comp + seg
    db = 256
    return pl.pallas_call(
        functools.partial(rows_kernel, sizes),
        grid=(D // db,),
        in_specs=[
            whole((2, local, width)),
            whole((2, local, width)),
            whole((seg, width)),
            pl.BlockSpec((1, mem, db), lambda j: (b, 0, j)),
            pl.BlockSpec((db, 4 * width), lambda j: (j, 0)),
        ],
        out_specs=[
            whole((local, 2 * width)),
            pl.BlockSpec((kept, db), lambda j: (0, j)),
            pl.BlockSpec((fresh, db), lambda j: (0, j)),
            pl.BlockSpec((8, db), lambda j: (0, j)),
        ],
        out_shape=[
            jax.ShapeDtypeStruct((local, 2 * width), BF16),
            jax.ShapeDtypeStruct((kept, D), BF16),
            jax.ShapeDtypeStruct((fresh, D), BF16),
            jax.ShapeDtypeStruct((8, D), F32),
        ],
        scratch_shapes=[pltpu.VMEM((local, 2 * width), BF16)],
        compiler_params=params(),
        cost_estimate=cost(3),
        name="rows_back",
    )(keep, got, gq, normed_mem, w)


def summed(refs, part):
    total = refs[0][part].astype(F32)
    for other in refs[1:]:
        total = total + other[part].astype(F32)
    return total


def context_kernel(sizes, parts, chained, *refs):
    grads = refs[:parts]
    comp, seg, ghid, gain = refs[parts : parts + 4]
    gcomp, gin, sums = refs[parts + 4 + (2 if chained else 0) :]
    rows = comp.shape[1]
    total = None
    for raw, part in ((comp, slice(0, rows)), (seg, slice(rows, None))):
        grad = summed(grads, part)
        xhat, r = standardize(raw[0].astype(F32))
        g = norm_back(grad, xhat, r, gain[...])
        part_sums = row_sums([grad * xhat, grad], D)
        if total is None:
            gcomp[0] = g
            total = part_sums
        else:
            gin[0] = ghid[...] + g
            total = total + part_sums
    sums[...] = total


def context_back(b, grads, comp, seg, ghid, gain, before, sizes):
    batch = comp.shape[0]
    kept = grads[0].shape[0]
    chained = before is not None
    n_comp, _, _, n_seg = sizes
    first = len(grads) + 4
    return pl.pallas_call(
        functools.partial(context_kernel, sizes, len(grads), chained),
        grid=(1,),
        in_specs=[whole((kept, D)) for _ in grads]
        + [stream(b, n_comp), stream(b, n_seg), whole((n_seg, D)), whole((1, D))]
        + ([pl.BlockSpec(memory_space=pl.ANY)] * 2 if chained else []),
        out_specs=[stream(b, n_comp), stream(b, n_seg), whole((8, D))],
        out_shape=[
            jax.ShapeDtypeStruct((batch, n_comp, D), F32),
            jax.ShapeDtypeStruct((batch, n_seg, D), F32),
            jax.ShapeDtypeStruct((8, D), F32),
        ],
        input_output_aliases={first: 0, first + 1: 1} if chained else {},
        compiler_params=params(),
        cost_estimate=cost(3),
        name="context_back",
    )(*grads, comp, seg, ghid, gain[None], *(before if chained else ()))


def fresh_kernel(batch, *refs):
    count = len(refs) - 4
    raw, gain, gfresh, sums = refs[count:]
    per = count // batch
    total = None
    for b in range(batch):
        grad = summed(refs[b * per : (b + 1) * per], slice(None))
        xhat, r = standardize(raw[b].astype(F32))
        rows = xhat.shape[0]
        g = norm_back(grad, xhat, r, gain[...])
        gfresh[b * rows : (b + 1) * rows] = g.astype(BF16)
        part_sums = row_sums([grad * xhat, grad, g.astype(BF16).astype(F32)], D)
        total = part_sums if total is None else total + part_sums
    sums[...] = total


def fresh_back(grads, raw, gain):
    batch, rows, _ = raw.shape
    flat = [g for pair in grads for g in pair]
    return pl.pallas_call(
        functools.partial(fresh_kernel, batch),
        grid=(1,),
        in_specs=[whole((rows, D)) for _ in flat] + [whole(raw.shape), whole((1, D))],
        out_specs=[whole((batch * rows, D)), whole((8, D))],
        out_shape=[
            jax.ShapeDtypeStruct((batch * rows, D), BF16),
            jax.ShapeDtypeStruct((8, D), F32),
        ],
        compiler_params=params(),
        cost_estimate=cost(2),
        name="fresh_back",
    )(*flat, raw, gain[None])


def table_kernel(keys, at, steps, w, out):
    seg = steps.shape[0] - keys
    first = pl.multiple_of((1 - at[0]) * seg, seg)
    out[...] = dot(steps[pl.ds(first, keys)], w[...], NN).astype(BF16)


def position_table(at, steps, w, keys, col, width):
    count = max(1, width // 256)
    cb = width // count
    return pl.pallas_call(
        functools.partial(table_kernel, keys),
        grid_spec=pltpu.PrefetchScalarGridSpec(
            num_scalar_prefetch=1,
            grid=(count,),
            in_specs=[
                whole(steps.shape),
                pl.BlockSpec((D, cb), lambda i, s: (0, col * count + i)),
            ],
            out_specs=pl.BlockSpec((keys, cb), lambda i, s: (0, i)),
        ),
        out_shape=jax.ShapeDtypeStruct((keys, width), BF16),
        compiler_params=params(),
        cost_estimate=cost(20),
        name="position_table",
    )(at, steps, w)


def split_out(acc, tier, rows, keep, send):
    v = acc.reshape(-1, 2, rows, acc.shape[1])
    first = tier == 0
    shape = keep.shape
    keep[...] = jnp.where(first, v[:, 0], v[:, 1]).reshape(shape).astype(BF16)
    send[...] = jnp.where(first, v[:, 1], v[:, 0]).reshape(shape).astype(BF16)


def grad_ffn_kernel(steps, n2, gpre, go, act, out):
    j = pl.program_id(0)

    @pl.when(j < steps)
    def _():
        out[...] = dot(n2[...], gpre[...], TN).astype(BF16)

    @pl.when(j >= steps)
    def _():
        out[...] = dot(go[...], act[...], TN).astype(BF16)


def grad_ffn(n2, gpre, go, act):
    rows, hidden = act.shape
    hb = min(512, hidden)
    steps = hidden // hb

    def block(first):
        return pl.BlockSpec(
            (rows, hb), lambda j: (0, jnp.clip(j - first, 0, steps - 1))
        )

    return pl.pallas_call(
        functools.partial(grad_ffn_kernel, steps),
        grid=(2 * steps,),
        in_specs=[whole((rows, D)), block(0), whole((rows, D)), block(steps)],
        out_specs=pl.BlockSpec((D, hb), lambda j: (0, j)),
        out_shape=jax.ShapeDtypeStruct((D, 2 * hidden), BF16),
        compiler_params=params(),
        cost_estimate=cost(30),
        name="grad_ffn",
    )(n2, gpre, go, act)


def fill(y, ys):
    rows = ys[0].shape[0]
    for k, part in enumerate(ys):
        y[k * rows : (k + 1) * rows] = part[...]


def grad_kv_kernel(batch, x, *refs):
    ys, (_, out, y) = refs[:batch], refs[batch:]
    fill(y, ys)
    out[...] = dot(x[...], y[...], TN).astype(BF16)


def grad_kv(x, ys, grads, col, width):
    every = x.shape[0]
    return pl.pallas_call(
        functools.partial(grad_kv_kernel, len(ys)),
        grid=(2,),
        in_specs=[whole(x.shape)]
        + [pl.BlockSpec((y.shape[0], width), lambda j: (0, j)) for y in ys]
        + [pl.BlockSpec(memory_space=pl.ANY)],
        out_specs=pl.BlockSpec((D, width), lambda j: (0, col + j)),
        scratch_shapes=[pltpu.VMEM((every, width), BF16)],
        out_shape=jax.ShapeDtypeStruct(grads.shape, BF16),
        input_output_aliases={1 + len(ys): 0},
        compiler_params=params(),
        cost_estimate=cost(8),
        name="grad_kv",
    )(x, *ys, grads)


def grad_rest_kernel(batch, at, normed, *refs):
    gq, gbr, att = (refs[k * batch : (k + 1) * batch] for k in range(3))
    steps, gtable, out, x, y = refs[3 * batch :]
    j = pl.program_id(0)
    tier = at[0]

    @pl.when(j == 0)
    def _():
        fill(x, [normed.at[k] for k in range(batch)])
        fill(y, gq)

    @pl.when(j == 1)
    def _():
        fill(x, gbr)
        fill(y, att)

    @pl.when(j < 2)
    def _():
        out[...] = dot(x[...], y[...], TN).astype(BF16)

    @pl.when(j == 2)
    def _():
        keys = gtable.shape[1]
        seg = steps.shape[0] - keys
        first = pl.multiple_of((1 - tier) * seg, seg)
        turned = dot(gtable[...].astype(BF16), steps[pl.ds(first, keys)], NN)
        out[...] = turned.astype(BF16).T


def grad_rest(at, normed, gq, gbr, att, steps, gtable, cols):
    seg, width = gq[0].shape
    batch, local, _ = normed.shape
    return pl.pallas_call(
        functools.partial(grad_rest_kernel, batch),
        grid_spec=pltpu.PrefetchScalarGridSpec(
            num_scalar_prefetch=1,
            grid=(3,),
            in_specs=[
                pl.BlockSpec((batch, seg, D), lambda j, s: (0, local // seg - 1, 0))
            ]
            + [whole((seg, width))] * batch
            + [whole((seg, D))] * batch
            + [whole((seg, width))] * batch
            + [whole(steps.shape), whole(gtable.shape)],
            out_specs=pl.BlockSpec((D, width), lambda j, s: (0, j)),
            scratch_shapes=[
                pltpu.VMEM((batch * seg, D), BF16),
                pltpu.VMEM((batch * seg, width), BF16),
            ],
        ),
        out_shape=jax.ShapeDtypeStruct((D, cols), BF16),
        compiler_params=params(),
        cost_estimate=cost(8),
        name="grad_rest",
    )(at, normed, *gq, *gbr, *att, steps, gtable)


def grad_conv_kernel(rows, at, taps, fresh, keep, send):
    split_out(dot(taps[...], fresh[...], TN), at[0], rows, keep, send)


def grad_conv(at, grouped, fresh, wide, rows):
    count = grouped.shape[0]
    return pl.pallas_call(
        functools.partial(grad_conv_kernel, rows),
        grid_spec=pltpu.PrefetchScalarGridSpec(
            num_scalar_prefetch=1,
            grid=(KW,),
            in_specs=[
                pl.BlockSpec((count, D), lambda j, s: (0, j)),
                pl.BlockSpec((count, wide), lambda j, s: (0, s[1])),
            ],
            out_specs=[pl.BlockSpec((D // 2, wide), lambda j, s: (0, j))] * 2,
        ),
        out_shape=[jax.ShapeDtypeStruct((D // 2, KW * wide), BF16)] * 2,
        compiler_params=params(),
        cost_estimate=cost(4),
        name="grad_conv",
    )(at, grouped, fresh)


def conv_kernel(taps, w, bias, out):
    k = pl.program_id(0)
    part = dot(taps[...], w[...], NN)

    @pl.when(k == 0)
    def _():
        out[...] = part + bias[...]

    @pl.when(k > 0)
    def _():
        out[...] += part


def compress(grouped, w, bias):
    count = grouped.shape[0]
    wide = bias.shape[0]
    return pl.pallas_call(
        conv_kernel,
        grid=(KW,),
        in_specs=[
            pl.BlockSpec((count, D), lambda j: (0, j)),
            pl.BlockSpec((D, wide), lambda j: (0, j)),
            whole((1, wide)),
        ],
        out_specs=whole((count, wide)),
        out_shape=jax.ShapeDtypeStruct((count, wide), F32),
        compiler_params=params(),
        cost_estimate=cost(3),
        name="compress",
    )(grouped, w, bias[None])


def distance_rows(first, count):
    half = D // 2
    freq = np.exp(np.arange(half) * (-2.0 * math.log(10000.0) / D))
    turned = (first - np.arange(count))[:, None] * freq[None, :]
    return np.concatenate([np.sin(turned), np.cos(turned)], axis=1).astype(
        ml_dtypes.bfloat16
    )


def col_sum(x):
    return jnp.sum(x, axis=tuple(range(x.ndim - 1)))


def ein(spec, a, b):
    return jnp.einsum(spec, a, b, preferred_element_type=F32)


def norm_rows(rows, gain, shift):
    return (standardize(rows.astype(F32))[0] * gain + shift).astype(BF16)


def shards(
    segment_input,
    memory,
    compressed,
    evicted,
    cotangent,
    seg_lengths,
    memory_fills,
    compressed_fills,
    conv_weight,
    conv_bias,
    norm1_gain,
    norm1_bias,
    query_weight,
    key_weight,
    value_weight,
    position_weight,
    content_bias,
    position_bias,
    out_weight,
    norm2_gain,
    norm2_bias,
    up_weight,
    up_bias,
    down_weight,
    down_bias,
):
    tier = lax.axis_index("tier")
    head = lax.axis_index("head")
    heads_n = lax.axis_size("head")
    batch, seg, _ = segment_input.shape
    mem = memory.shape[1]
    comp = compressed.shape[1]
    fresh = evicted.shape[1] // KW
    sizes = (comp, fresh, mem, seg)
    width = query_weight.shape[1]
    wide = conv_weight.shape[2]
    hidden = up_weight.shape[1]
    keys = 2 * (comp + fresh + mem + seg)
    rows = query_weight.shape[0]
    streams = range(batch)
    at = jnp.concatenate(
        [
            jnp.stack([tier, head]).astype(jnp.int32),
            jnp.stack([compressed_fills, memory_fills, seg_lengths], 1).reshape(-1),
        ]
    )


    conv_z = gather_z(jnp.concatenate([conv_weight[k] for k in range(KW)], 1))
    out_t = head_gather(out_weight.T)
    full = out_t.shape[1]
    attn_pack = jnp.concatenate(
        [key_weight, value_weight, query_weight, position_weight], 1
    )
    ffn_pack = jnp.concatenate([out_t, up_weight, down_weight.T], 1)
    attn_z = gather_z(after(attn_pack, conv_z, out_t))
    ffn_w = lax.all_gather(
        after(ffn_pack, conv_z), ("dp", "tier"), axis=0, tiled=True
    )
    conv_blocks = gather_yt(conv_z)
    conv_blocks[0] = after(conv_blocks[0], out_t)
    conv_w = place(conv_blocks)

    n_comp = norm_rows(compressed, norm1_gain, norm1_bias)
    n_mem = norm_rows(memory, norm1_gain, norm1_bias)
    n_seg = norm_rows(segment_input, norm1_gain, norm1_bias)
    grouped = evicted.reshape(batch * fresh, KW * D)
    fresh_part = compress(grouped, conv_w, conv_bias).astype(BF16)
    fresh_rows = head_gather(fresh_part.reshape(batch, fresh, wide))
    n_fresh = norm_rows(fresh_rows, norm1_gain, norm1_bias)
    attn_blocks = gather_yt(attn_z)
    attn_blocks[0] = after(attn_blocks[0], fresh_part)
    attn_w = place(attn_blocks)

    normed, kv, q = project(n_comp, n_fresh, n_mem, n_seg, attn_w)
    kv_other = swap(kv, "tier")
    steps = jnp.asarray(distance_rows(keys - 1, keys + seg))
    table = position_table(at, steps, after(attn_w, kv), keys, 3, width)
    atts, probs, others = [], [], []
    for b in streams:
        q_b = after(q, *(others[-2:-1] + atts[-1:])) if b else after(q, table)
        att, p = attend(
            b, at, q_b, kv, kv_other, table, content_bias, position_bias, sizes
        )
        atts.append(att)
        probs.append(p)
        if heads_n == 2:
            others.append(swap(att, "head"))
        else:
            others.append(lax.all_gather(att, "head", axis=1, tiled=True))

    def over_head(x):
        if heads_n == 2:
            return [x, swap(x, "head")]
        return [lax.psum(x, "head")]

    if heads_n == 2:
        pairs = [v for pair in zip(atts, others) for v in pair]
    else:
        pairs = others
    hid, n2, go, act, gpre, up_sums, out_sums, *halves = feed_forward(
        at,
        pairs,
        segment_input,
        cotangent,
        ffn_w,
        full,
        norm2_gain,
        norm2_bias,
        up_bias,
    )
    twos = [over_head(halves[0])]
    g_ffn = grad_ffn(n2, gpre, go, act)
    g_ffn_s = lax.psum_scatter(
        g_ffn, ("dp", "tier"), scatter_dimension=0, tiled=True
    )

    ghids, gbrs, gqs, keeps, gots = [], [], [], [], []
    gkvs, parts, fparts, downs = [], [], [], []
    bias_sums, mem_sums, mid_rows = 0, 0, 0
    gtable = None
    last = g_ffn

    def rows_of(b, *others):
        gq = after(gqs[b], *others)
        gkv, part, fpart, sums = rows_back(
            b, keeps[b], gots[b], gq, n_mem, attn_w, sizes
        )
        gkvs.append(gkv)
        fparts.append(over_head(fpart))
        parts.append(over_head(part) if b == 0 else part)
        return sums[:2], part

    for b in streams:
        if b > 1:
            sums, last = rows_of(b - 2, last)
            mem_sums = mem_sums + sums
        if b < batch - 1:
            twos.append(over_head(after(halves[b + 1], twos[b][-1])))
        ghid, gbr, sums, gq, keep, send, gtable, gbias = attend_back(
            b,
            at,
            twos[b],
            hid,
            after(go, last),
            norm2_gain,
            ffn_w,
            probs[b],
            q,
            kv,
            kv_other,
            table,
            content_bias,
            position_bias,
            sizes,
            gtable,
        )
        last = gq
        ghids.append(ghid)
        gbrs.append(gbr)
        gqs.append(gq)
        keeps.append(keep)
        gots.append(swap(send, "tier"))
        if 0 < b:
            downs.append(over_head(after(halves[batch + b - 1], gq)))
        mid_rows = mid_rows + sums
        bias_sums = bias_sums + gbias
    for b in range(max(batch - 2, 0), batch):
        sums, last = rows_of(b, last)
        mem_sums = mem_sums + sums
    early = [pair[-1] for pair in fparts[:-1]]
    gq_0 = after(gqs[0], last, parts[0][-1], *early)
    grads = grad_rest(
        at, normed, [gq_0] + gqs[1:], gbrs, atts, steps, gtable, 5 * width
    )
    for b in range(1, batch):
        parts[b] = over_head(after(parts[b], fparts[-1][-1]))
    fresh_grad, fresh_sums = fresh_back(
        fparts, after(fresh_rows, grads), norm1_gain
    )
    keep, send = grad_conv(at, grouped, fresh_grad, wide, rows)
    grads = grad_kv(after(normed, keep, g_ffn_s).reshape(-1, D), gkvs, grads, 3, width)
    grads_s = lax.psum_scatter(
        grads, ("dp", "tier"), scatter_dimension=0, tiled=True
    )
    got = swap(send, "tier")
    row_totals = fresh_sums[:2]
    before = None

    def context_of(b, *others):
        return context_back(
            b,
            parts[b],
            compressed,
            segment_input,
            after(ghids[b], *others),
            norm1_gain,
            before,
            sizes,
        )

    mine, theirs = halve(keep, after(got, grads))
    other = swap(theirs, "dp")
    *before, sums = context_of(0, theirs)
    row_totals = row_totals + sums[:2]
    added = add_low(mine, other)
    conv_all = z_exchange(added)
    for b in range(1, batch):
        *before, sums = context_of(
            b, before[1], conv_all if b == batch - 1 else added
        )
        row_totals = row_totals + sums[:2]
    grad_comp, grad_in = before
    g_conv = jnp.sum(after(conv_all, grad_in).astype(F32), axis=0)
    g_conv = jnp.stack([g_conv[:, k * wide : (k + 1) * wide] for k in range(KW)])
    mem_sums = sum(over_head(after(mem_sums, grad_in)))
    downs.append(over_head(after(halves[-1], grad_in)))
    grads_s = after(grads_s, conv_all)
    g_q, g_out, g_pos, g_k, g_v = (
        grads_s[:, k * width : (k + 1) * width].astype(F32) for k in range(5)
    )

    outs = []
    for b in streams:
        out = hid[b * seg : (b + 1) * seg] + down_bias
        for x in downs[b]:
            out = out + x.astype(F32)
        outs.append(out.astype(BF16))
    output = jnp.stack(outs)
    mem_gain = (mem_sums[0] - norm1_bias * mem_sums[1]) / norm1_gain
    fresh_sum = lax.dynamic_slice_in_dim(fresh_sums[2], head * wide, wide, 0)
    sums = small_sum(
        [
            mid_rows[0],
            mid_rows[1],
            up_sums[0],
            out_sums[0],
            fresh_sum,
            row_totals[0] + mem_gain,
            row_totals[1] + mem_sums[1],
            bias_sums[:, 0],
            bias_sums[:, 1],
        ]
    )
    return (
        output,
        grad_in,
        grad_comp,
        g_conv,
        sums[4],
        sums[5],
        sums[6],
        g_q,
        g_k,
        g_v,
        g_pos,
        sums[7],
        sums[8],
        g_out.T,
        sums[0],
        sums[1],
        g_ffn_s[:, :hidden].astype(F32),
        sums[2],
        g_ffn_s[:, hidden:].T.astype(F32),
        sums[3],
    )


def solution(mesh):
    rows = P("dp", "tier", None)
    by_row = P(("dp", "tier"), "head")
    by_col = P("head", ("dp", "tier"))
    conv = P(None, ("dp", "tier"), "head")
    heads = P("head", None)
    placed = (
        (rows,) * 5
        + (P("dp"),) * 3
        + (conv, P("head"), P(), P())
        + (by_row,) * 4
        + (heads, heads, by_col, P(), P(), by_row, P("head"), by_col, P())
    )
    results = (
        (rows,) * 3
        + (conv, P("head"), P(), P())
        + (by_row,) * 4
        + (heads, heads, by_col, P(), P(), by_row, P("head"), by_col, P())
    )
    return jax.shard_map(
        shards, mesh=mesh, in_specs=placed, out_specs=results, check_vma=False
    )
```

```python
import functools
import math

import jax
import jax.numpy as jnp
import ml_dtypes
import numpy as np
from jax import lax
from jax.experimental import pallas as pl
from jax.experimental.pallas import tpu as pltpu
from jax.sharding import PartitionSpec as P

D = 1024
MEM = 512
CMEM = 512
KW = 3
OLDC = 384
EPS = 1e-05
NEG = -1e30
F32 = jnp.float32
BF16 = jnp.bfloat16


def swap(x, axis, step=1):
    n = lax.axis_size(axis)
    return lax.ppermute(x, axis, [(i, i ^ step) for i in range(n)])


def after(x, *others):
    return lax.optimization_barrier((x, *others))[0]


def z_exchange(x):
    n = lax.axis_size("dp")
    groups = [[z * 2 + y for z in range(n // 2)] for y in range(2)]
    return lax.all_to_all(x, "dp", 0, 0, axis_index_groups=groups, tiled=True)


def head_gather(x):
    if lax.axis_size("head") == 2:
        other = swap(x, "head")
        first = lax.axis_index("head") == 0
        return jnp.concatenate(
            [jnp.where(first, x, other), jnp.where(first, other, x)], axis=-1
        )
    return lax.all_gather(x, "head", axis=x.ndim - 1, tiled=True)


def place_kernel(at_ref, b0, b1, b2, b3, out, sems):
    y, t = at_ref[0], at_ref[1]
    copies = []
    for k, block in enumerate((b0, b1, b2, b3)):
        yy = 1 - y if k % 2 else y
        tt = 1 - t if k // 2 else t
        copies.append(pltpu.make_async_copy(block, out.at[:, yy, tt], sems.at[k]))
    for copy in copies:
        copy.start()
    for copy in copies:
        copy.wait()


def gather_z(x):
    zn = lax.axis_size("dp") // 2
    return z_exchange(jnp.broadcast_to(x[None], (zn,) + x.shape))


def gather_yt(over_z):
    other = swap(over_z, "dp")
    return [over_z, other, swap(over_z, "tier"), swap(other, "tier")]


def place(blocks):
    zn, rows, cols = blocks[0].shape
    shape = (zn, 2, 2, rows, cols)
    at = jnp.stack([lax.axis_index("dp") % 2, lax.axis_index("tier")])
    out = pl.pallas_call(
        place_kernel,
        grid_spec=pltpu.PrefetchScalarGridSpec(
            num_scalar_prefetch=1,
            grid=(1,),
            in_specs=[pl.BlockSpec(memory_space=pl.ANY)] * 4,
            out_specs=pl.BlockSpec(shape, lambda i, s: (0, 0, 0, 0, 0)),
            scratch_shapes=[pltpu.SemaphoreType.DMA((4,))],
        ),
        out_shape=jax.ShapeDtypeStruct(shape, blocks[0].dtype),
        compiler_params=pltpu.CompilerParams(vmem_limit_bytes=60 << 20),
        cost_estimate=cost(3),
        name="place",
    )(at.astype(jnp.int32), *blocks)
    return out.reshape(zn * 4 * rows, cols)


def add_low(a, b):
    return (a.astype(F32) + b.astype(F32)).astype(BF16)


def halve(keep, got):
    zn = lax.axis_size("dp") // 2
    y = lax.axis_index("dp") % 2
    shape = (zn, 2, keep.shape[0] // (2 * zn), keep.shape[1])
    keep, got = keep.reshape(shape), got.reshape(shape)

    def pick(k):
        a, b = (lax.dynamic_index_in_dim(v, k, 1, keepdims=False) for v in (keep, got))
        return add_low(a, b)

    return pick(y), pick(1 - y)


def small_sum(parts):
    flat = jnp.concatenate([p.reshape(-1) for p in parts])
    pad = -flat.shape[0] % 1024
    flat = jnp.pad(flat, (0, pad)).reshape(-1, 128)
    n = lax.axis_size("dp")
    if n & (n - 1):
        flat = lax.psum(flat, ("dp", "tier"))
    else:
        flat = flat + swap(flat, "tier")
        step = 1
        while step < n:
            flat = flat + swap(flat, "dp", step)
            step *= 2
    flat = flat.reshape(-1)
    out, at = [], 0
    for p in parts:
        out.append(flat[at : at + p.size].reshape(p.shape))
        at += p.size
    return out


def dot(a, b, contract):
    return lax.dot_general(a, b, (contract, ((), ())), preferred_element_type=F32)


NN = ((1,), (0,))
NT = ((1,), (1,))
TN = ((0,), (0,))


def params(mib=60):
    return pltpu.CompilerParams(vmem_limit_bytes=mib << 20)


def cost(us):
    return pl.CostEstimate(
        flops=int(us * 1.15e9), bytes_accessed=1024, transcendentals=0
    )


def whole(shape):
    return pl.BlockSpec(shape, lambda *i: (0,) * len(shape))


def stream(b, rows, cols=D):
    return pl.BlockSpec((1, rows, cols), lambda *i: (b, 0, 0))


def key_pieces(sizes):
    comp, fresh, mem, seg = sizes
    return (
        (0, 0, comp),
        (comp, OLDC, fresh),
        (comp + fresh, CMEM, mem),
        (comp + fresh + mem, CMEM + MEM, seg),
    )


def in_order(full, own, other, tier, sizes):
    for row, pos, rows in key_pieces(sizes):
        mine = pl.multiple_of(pos + tier * rows, rows)
        theirs = pl.multiple_of(pos + (1 - tier) * rows, rows)
        full[pl.ds(mine, rows)] = own[0, row : row + rows]
        full[pl.ds(theirs, rows)] = other[0, row : row + rows]


def project_kernel(comp, fresh, mem, seg, w, normed, kv, q):
    at = 0
    for piece in (comp, fresh, mem, seg):
        rows = piece.shape[1]
        normed[0, at : at + rows] = piece[0]
        at += rows
    width = q.shape[2]
    kv[0] = dot(normed[0], w[:, : 2 * width], NN).astype(BF16)
    first = at - seg.shape[1]
    q[0] = dot(normed[0, first:], w[:, 2 * width : 3 * width], NN).astype(BF16)


def project(comp, fresh, mem, seg, w):
    batch = comp.shape[0]
    width = w.shape[1] // 4
    pieces = (comp, fresh, mem, seg)
    rows = sum(p.shape[1] for p in pieces)

    def block(n, cols=D):
        return pl.BlockSpec((1, n, cols), lambda b: (b, 0, 0))

    shapes = ((rows, D), (rows, 2 * width), (seg.shape[1], width))
    return pl.pallas_call(
        project_kernel,
        grid=(batch,),
        in_specs=[block(p.shape[1]) for p in pieces] + [whole(w.shape)],
        out_specs=[block(*shape) for shape in shapes],
        out_shape=[jax.ShapeDtypeStruct((batch,) + shape, BF16) for shape in shapes],
        compiler_params=params(),
        cost_estimate=cost(50),
        name="project",
    )(*pieces, w)


def forward_kernel(
    b, sizes, at, q, k_own, k_other, v_own, v_other, table, cb, pb, att, probs, kf, vf
):
    tier = at[0]
    comp_fill, mem_fill, seg_len = at[2 + 3 * b], at[3 + 3 * b], at[4 + 3 * b]
    rows = q.shape[1]
    keys = kf.shape[0]
    in_order(kf, k_own, k_other, tier, sizes)
    in_order(vf, v_own, v_other, tier, sizes)
    query = q[0].astype(F32)
    content_q = (query + cb[0]).astype(BF16)
    position_q = (query + pb[0]).astype(BF16)
    scale = 1.0 / math.sqrt(q.shape[2])
    relative = dot(position_q, table[...], NT)
    relative = pltpu.roll(relative, keys - rows + 1, 1, stride=1, stride_axis=0)
    scores = (dot(content_q, kf[...], NT) + relative) * scale
    start = CMEM + MEM
    j = lax.broadcasted_iota(jnp.int32, (1, keys), 1)
    lowest = jnp.where(
        j < CMEM, CMEM - comp_fill, jnp.where(j < start, start - mem_fill, start)
    )
    beyond = jnp.where(j < start, start, start + seg_len)
    open_col = (j >= lowest) & (j < beyond)
    bias = jnp.where(open_col, 0.0, NEG)
    i = lax.broadcasted_iota(jnp.int32, (rows, keys), 0) + tier * rows
    jj = lax.broadcasted_iota(jnp.int32, (rows, keys), 1) - start
    masked = jnp.where(jj <= i, scores + bias, NEG)
    peak = jnp.max(masked, axis=-1, keepdims=True)
    e = jnp.exp(masked - peak)
    total = jnp.sum(e, axis=-1, keepdims=True)
    p = (e * (1.0 / total)).astype(BF16)
    probs[0] = p
    att[...] = dot(p, vf[...], NN).astype(BF16)


def attend(b, at, q, kv, kv_other, table, cb, pb, sizes):
    _, rows, width = q.shape
    heads = cb.shape[0]
    hd = width // heads
    keys_local = kv.shape[1]
    keys = 2 * keys_local

    def col(off):
        return pl.BlockSpec((1, keys_local, hd), lambda h, s: (b, 0, h + off))

    def bias():
        return pl.BlockSpec((1, 1, hd), lambda h, s: (h, 0, 0))

    return pl.pallas_call(
        functools.partial(forward_kernel, b, sizes),
        grid_spec=pltpu.PrefetchScalarGridSpec(
            num_scalar_prefetch=1,
            grid=(heads,),
            in_specs=[
                pl.BlockSpec((1, rows, hd), lambda h, s: (b, 0, h)),
                col(0),
                col(0),
                col(heads),
                col(heads),
                pl.BlockSpec((keys, hd), lambda h, s: (0, h)),
                bias(),
                bias(),
            ],
            out_specs=[
                pl.BlockSpec((rows, hd), lambda h, s: (0, h)),
                pl.BlockSpec((1, rows, keys), lambda h, s: (h, 0, 0)),
            ],
            scratch_shapes=[pltpu.VMEM((keys, hd), BF16), pltpu.VMEM((keys, hd), BF16)],
        ),
        out_shape=[
            jax.ShapeDtypeStruct((rows, width), BF16),
            jax.ShapeDtypeStruct((heads, rows, keys), BF16),
        ],
        compiler_params=params(),
        cost_estimate=cost(20),
        name="attend",
    )(at, q, kv, kv_other, kv, kv_other, table, cb[:, None], pb[:, None])


def standardize(rows):
    mean = jnp.mean(rows, axis=-1, keepdims=True)
    centred = rows - mean
    var = jnp.mean(centred * centred, axis=-1, keepdims=True)
    r = lax.rsqrt(var + EPS)
    return centred * r, r


def norm_back(grad, xhat, r, gain):
    g = grad * gain
    return r * (
        g
        - jnp.mean(g, axis=-1, keepdims=True)
        - xhat * jnp.mean(g * xhat, axis=-1, keepdims=True)
    )


def row_sums(values, width):
    sums = [jnp.sum(v, axis=0, keepdims=True) for v in values]
    return jnp.concatenate(sums + [jnp.zeros((8 - len(sums), width), F32)], axis=0)


def ffn_kernel(batch, parts, full, at, *refs):
    count = batch * parts
    atts = refs[:count]
    x, cot, gain, shift, up_b, w = refs[count : count + 6]
    outs = refs[count + 6 :]
    kept_out, (sums_up, sums_out) = outs[:5], outs[5:7]
    twos, ffns = outs[7 : 7 + batch], outs[7 + batch : 7 + 2 * batch]
    kept, (wv, w_sem, sem) = outs[7 + 2 * batch : -3], outs[-3:]
    hidden, n2, go, act, gpre = kept
    hid = act.shape[1]
    hb = min(512, hid)
    steps = hid // hb
    tier, head = at[0], at[1]
    rows = x.shape[1]

    def fetch(k, first, cols):
        part = slice(first, first + cols)
        return pltpu.make_async_copy(w.at[:, part], wv.at[:, part], w_sem.at[k])

    copies = [fetch(0, 0, full), fetch(1, full, hid), fetch(2, full + hid, hid)]
    for copy in copies:
        copy.start()
    going = []

    def give(k, cols):
        copy = pltpu.make_async_copy(
            kept[k].at[:, cols], kept_out[k].at[:, cols], sem.at[len(going)]
        )
        copy.start()
        going.append(copy)

    every = slice(0, D)
    total = None
    for b in range(batch):
        row = lax.broadcasted_iota(jnp.int32, (rows, 1), 0) + tier * rows
        masked = jnp.where(row < at[4 + 3 * b], cot[b].astype(F32), 0.0)
        go[b * rows : (b + 1) * rows] = masked.astype(BF16)
        sums = row_sums([masked], D)
        total = sums if total is None else total + sums
    sums_out[...] = total
    give(2, every)
    copies[0].wait()
    if parts == 2:
        first = head == 0
        att = jnp.concatenate(
            [
                jnp.concatenate(
                    [
                        jnp.where(first, atts[2 * b][...], atts[2 * b + 1][...]),
                        jnp.where(first, atts[2 * b + 1][...], atts[2 * b][...]),
                    ],
                    axis=1,
                )
                for b in range(batch)
            ],
            axis=0,
        )
    else:
        att = jnp.concatenate([a[...] for a in atts], axis=0)
    h = x[...].reshape(batch * rows, D).astype(F32) + dot(att, wv[:, :full], NT)
    hidden[...] = h
    give(0, every)
    xhat, _ = standardize(h)
    n2[...] = (xhat * gain[...] + shift[...]).astype(BF16)
    give(1, every)
    copies[1].wait()
    copies[2].wait()
    c = math.sqrt(2.0 / math.pi)
    ck = c * 0.044715
    for j in range(steps):
        cols = slice(j * hb, (j + 1) * hb)
        up = wv[:, full + j * hb : full + (j + 1) * hb]
        down = wv[:, full + hid + j * hb : full + hid + (j + 1) * hb]
        pre = dot(n2[...], up, NN) + up_b[:, cols]
        g_act = dot(go[...], down, NN)
        sq = pre * pre
        half = 0.5 + 0.5 * jnp.tanh(pre * (c + ck * sq))
        a = pre * half
        slope = half + a * (1.0 - half) * (2 * c + 6 * ck * sq)
        g = (g_act * slope).astype(BF16)
        act[:, cols] = a.astype(BF16)
        gpre[:, cols] = g
        sums_up[:, cols] = row_sums([g.astype(F32)], hb)
        give(3, cols)
        give(4, cols)
    for outs_of, k, first in ((twos, 4, full), (ffns, 3, full + hid)):
        product = dot(kept[k][...], wv[:, first : first + hid], NT).astype(BF16)
        for b in range(batch):
            outs_of[b][...] = product[b * rows : (b + 1) * rows]
    for copy in going:
        copy.wait()


def feed_forward(at, atts, x, cot, w_ffn, full, gain, shift, up_b):
    batch, rows, _ = x.shape
    hidden_n = (w_ffn.shape[1] - full) // 2
    steps = hidden_n // min(512, hidden_n)
    every = batch * rows
    anywhere = pl.BlockSpec(memory_space=pl.ANY)
    kept = [(D, F32), (D, BF16), (D, BF16), (hidden_n, BF16), (hidden_n, BF16)]
    return pl.pallas_call(
        functools.partial(ffn_kernel, batch, len(atts) // batch, full),
        grid_spec=pltpu.PrefetchScalarGridSpec(
            num_scalar_prefetch=1,
            grid=(1,),
            in_specs=[whole(a.shape) for a in atts]
            + [whole(x.shape)] * 2
            + [whole((1, D)), whole((1, D)), whole((1, hidden_n)), anywhere],
            out_specs=[anywhere] * 5
            + [whole((8, hidden_n)), whole((8, D))]
            + [whole((rows, D))] * (2 * batch),
            scratch_shapes=[pltpu.VMEM((every, n), dtype) for n, dtype in kept]
            + [
                pltpu.VMEM(w_ffn.shape, BF16),
                pltpu.SemaphoreType.DMA((3,)),
                pltpu.SemaphoreType.DMA((3 + 2 * steps,)),
            ],
        ),
        out_shape=[jax.ShapeDtypeStruct((every, n), dtype) for n, dtype in kept]
        + [jax.ShapeDtypeStruct((8, hidden_n), F32), jax.ShapeDtypeStruct((8, D), F32)]
        + [jax.ShapeDtypeStruct((rows, D), BF16)] * (2 * batch),
        compiler_params=params(),
        cost_estimate=cost(50),
        name="feed_forward",
    )(at, *atts, x, cot, gain[None], shift[None], up_b[None], w_ffn)


def backward_kernel(sizes, parts, chained, at, *refs):
    twos, refs = refs[:parts], refs[parts:]
    hidden, go, gain, w = refs[:4]
    (probs, q, k_own, k_other, v_own, v_other, table, cb, pb) = refs[4:13]
    refs = refs[13:]
    if chained:
        before, refs = refs[0], refs[1:]
    ghid, gbr, sums, gq, keep, send, gtable, gbias, kf, vf, gk, gatt = refs
    tier = at[0]
    step = pl.program_id(0)
    rows, hd = q.shape[1], q.shape[2]

    @pl.when(step == 0)
    def _():
        grad = summed(twos, slice(None))
        xhat, r = standardize(hidden[...])
        g = go[...].astype(F32) + norm_back(grad, xhat, r, gain[...])
        ghid[...] = g
        low = g.astype(BF16)
        gbr[...] = low
        out = dot(low, w[...], NN).astype(BF16)
        for k in range(gatt.shape[0]):
            gatt[k] = out[:, k * hd : (k + 1) * hd]
        sums[...] = row_sums([grad * xhat, grad], D)

    @pl.when(step > 0)
    def _():
        in_order(kf, k_own, k_other, tier, sizes)
        in_order(vf, v_own, v_other, tier, sizes)
        query = q[0].astype(F32)
        content_q = (query + cb[0]).astype(BF16)
        position_q = (query + pb[0]).astype(BF16)
        scale = 1.0 / math.sqrt(hd)
        ga = gatt[step - 1]
        p_low = probs[0]
        p = p_low.astype(F32)
        gp = dot(ga, vf[...], NT)
        row_dot = jnp.sum(p * gp, axis=-1, keepdims=True)
        ds = (p * (gp - row_dot)).astype(BF16)

        def hand_out(which, value):
            gk[...] = value.astype(BF16)
            for row, pos, size in key_pieces(sizes):
                mine = pl.multiple_of(pos + tier * size, size)
                theirs = pl.multiple_of(pos + (1 - tier) * size, size)
                keep[which, row : row + size] = gk[pl.ds(mine, size)]
                send[which, row : row + size] = gk[pl.ds(theirs, size)]

        hand_out(0, (dot(content_q, ds, TN) * scale).T)
        hand_out(1, dot(ga, p_low, TN).T)
        g_content = dot(ds, kf[...], NN) * scale
        r = lax.broadcasted_iota(jnp.int32, (rows, rows), 0)
        c = lax.broadcasted_iota(jnp.int32, (rows, rows), 1)
        flip = jnp.where(r + c == rows - 1, 1.0, 0.0).astype(BF16)
        ds_flip = dot(flip, ds, NN)
        skewed = pltpu.roll(ds_flip, 0, 1, stride=1, stride_axis=0).astype(BF16)
        position_flip = dot(flip, position_q, NN).astype(BF16)
        g_table = dot(position_flip, skewed, TN) * scale
        g_flip = dot(skewed, table[...], NN) * scale
        high = g_flip.astype(BF16)
        low = (g_flip - high.astype(F32)).astype(BF16)
        g_position = dot(flip, high, NN) + dot(flip, low, NN)
        gq[...] = (g_content + g_position).astype(BF16)
        gbias[0] = row_sums([g_content, g_position], hd)
        if chained:
            g_table = g_table + before[...]
        gtable[...] = g_table


def attend_back(
    b, at, twos, hidden, go, gain, w, probs, q, kv, kv_other, table, cb, pb, sizes, before
):
    _, rows, width = q.shape
    heads = cb.shape[0]
    hd = width // heads
    keys_local = kv.shape[1]
    keys = 2 * keys_local
    chained = before is not None

    def of(h):
        return jnp.maximum(h - 1, 0)

    def col(off):
        return pl.BlockSpec((1, keys_local, hd), lambda h, s: (b, 0, of(h) + off))

    def half():
        return pl.BlockSpec((2, keys_local, hd), lambda h, s: (0, 0, of(h)))

    def bias():
        return pl.BlockSpec((1, 1, hd), lambda h, s: (of(h), 0, 0))

    def turned():
        return pl.BlockSpec((hd, keys), lambda h, s: (of(h), 0))

    def own_rows():
        return pl.BlockSpec((rows, D), lambda h, s: (b, 0))

    args = [at, *twos, hidden, go, gain[None], w]
    args += [probs, q, kv, kv_other, kv, kv_other, table]
    args += [cb[:, None], pb[:, None]]
    return pl.pallas_call(
        functools.partial(backward_kernel, sizes, len(twos), chained),
        grid_spec=pltpu.PrefetchScalarGridSpec(
            num_scalar_prefetch=1,
            grid=(1 + heads,),
            in_specs=[whole((rows, D)) for _ in twos]
            + [
                own_rows(),
                own_rows(),
                whole((1, D)),
                pl.BlockSpec((D, width), lambda h, s: (0, s[1])),
                pl.BlockSpec((1, rows, keys), lambda h, s: (of(h), 0, 0)),
                pl.BlockSpec((1, rows, hd), lambda h, s: (b, 0, of(h))),
                col(0),
                col(0),
                col(heads),
                col(heads),
                pl.BlockSpec((keys, hd), lambda h, s: (0, of(h))),
                bias(),
                bias(),
            ]
            + ([turned()] if chained else []),
            out_specs=[
                whole((rows, D)),
                whole((rows, D)),
                whole((8, D)),
                pl.BlockSpec((rows, hd), lambda h, s: (0, of(h))),
                half(),
                half(),
                turned(),
                pl.BlockSpec((1, 8, hd), lambda h, s: (of(h), 0, 0)),
            ],
            scratch_shapes=[pltpu.VMEM((keys, hd), BF16)] * 3
            + [pltpu.VMEM((heads, rows, hd), BF16)],
        ),
        out_shape=[
            jax.ShapeDtypeStruct((rows, D), F32),
            jax.ShapeDtypeStruct((rows, D), BF16),
            jax.ShapeDtypeStruct((8, D), F32),
            jax.ShapeDtypeStruct((rows, width), BF16),
            jax.ShapeDtypeStruct((2, keys_local, width), BF16),
            jax.ShapeDtypeStruct((2, keys_local, width), BF16),
            jax.ShapeDtypeStruct((width, keys), F32),
            jax.ShapeDtypeStruct((heads, 8, hd), F32),
        ],
        compiler_params=params(),
        cost_estimate=cost(50),
        name="attend_back",
    )(*args, *([before] if chained else []))


def rows_kernel(sizes, keep, got, gq, normed_mem, w, gkv, part, fpart, sums, both):
    comp, fresh, mem, seg = sizes
    width = gq.shape[1]

    @pl.when(pl.program_id(0) == 0)
    def _():
        for k in range(2):
            total = keep[k].astype(F32) + got[k].astype(F32)
            both[:, k * width : (k + 1) * width] = total.astype(BF16)
        gkv[...] = both[...]

    low = comp + fresh
    split = low + mem
    grad = dot(both[...], w[:, : 2 * width], NT)
    part[:comp] = grad[:comp].astype(BF16)
    fpart[...] = grad[comp:low].astype(BF16)
    part[comp:] = (
        grad[split:] + dot(gq[...], w[:, 2 * width : 3 * width], NT)
    ).astype(BF16)
    g_mem = grad[low:split]
    sums[...] = row_sums([g_mem * normed_mem[0].astype(F32), g_mem], g_mem.shape[1])


def rows_back(b, keep, got, gq, normed_mem, w, sizes):
    width = gq.shape[1]
    local = keep.shape[1]
    comp, fresh, mem, seg = sizes
    kept = comp + seg
    db = D
    return pl.pallas_call(
        functools.partial(rows_kernel, sizes),
        grid=(D // db,),
        in_specs=[
            whole((2, local, width)),
            whole((2, local, width)),
            whole((seg, width)),
            pl.BlockSpec((1, mem, db), lambda j: (b, 0, j)),
            pl.BlockSpec((db, 4 * width), lambda j: (j, 0)),
        ],
        out_specs=[
            whole((local, 2 * width)),
            pl.BlockSpec((kept, db), lambda j: (0, j)),
            pl.BlockSpec((fresh, db), lambda j: (0, j)),
            pl.BlockSpec((8, db), lambda j: (0, j)),
        ],
        out_shape=[
            jax.ShapeDtypeStruct((local, 2 * width), BF16),
            jax.ShapeDtypeStruct((kept, D), BF16),
            jax.ShapeDtypeStruct((fresh, D), BF16),
            jax.ShapeDtypeStruct((8, D), F32),
        ],
        scratch_shapes=[pltpu.VMEM((local, 2 * width), BF16)],
        compiler_params=params(),
        cost_estimate=cost(3),
        name="rows_back",
    )(keep, got, gq, normed_mem, w)


def summed(refs, part):
    total = refs[0][part].astype(F32)
    for other in refs[1:]:
        total = total + other[part].astype(F32)
    return total


def context_kernel(sizes, parts, chained, *refs):
    grads = refs[:parts]
    comp, seg, ghid, gain = refs[parts : parts + 4]
    gcomp, gin, sums = refs[parts + 4 + (2 if chained else 0) :]
    rows = comp.shape[1]
    total = None
    for raw, part in ((comp, slice(0, rows)), (seg, slice(rows, None))):
        grad = summed(grads, part)
        xhat, r = standardize(raw[0].astype(F32))
        g = norm_back(grad, xhat, r, gain[...])
        part_sums = row_sums([grad * xhat, grad], D)
        if total is None:
            gcomp[0] = g
            total = part_sums
        else:
            gin[0] = ghid[...] + g
            total = total + part_sums
    sums[...] = total


def context_back(b, grads, comp, seg, ghid, gain, before, sizes):
    batch = comp.shape[0]
    kept = grads[0].shape[0]
    chained = before is not None
    n_comp, _, _, n_seg = sizes
    first = len(grads) + 4
    return pl.pallas_call(
        functools.partial(context_kernel, sizes, len(grads), chained),
        grid=(1,),
        in_specs=[whole((kept, D)) for _ in grads]
        + [stream(b, n_comp), stream(b, n_seg), whole((n_seg, D)), whole((1, D))]
        + ([pl.BlockSpec(memory_space=pl.ANY)] * 2 if chained else []),
        out_specs=[stream(b, n_comp), stream(b, n_seg), whole((8, D))],
        out_shape=[
            jax.ShapeDtypeStruct((batch, n_comp, D), F32),
            jax.ShapeDtypeStruct((batch, n_seg, D), F32),
            jax.ShapeDtypeStruct((8, D), F32),
        ],
        input_output_aliases={first: 0, first + 1: 1} if chained else {},
        compiler_params=params(),
        cost_estimate=cost(3),
        name="context_back",
    )(*grads, comp, seg, ghid, gain[None], *(before if chained else ()))


def fresh_kernel(batch, *refs):
    count = len(refs) - 4
    raw, gain, gfresh, sums = refs[count:]
    per = count // batch
    total = None
    for b in range(batch):
        grad = summed(refs[b * per : (b + 1) * per], slice(None))
        xhat, r = standardize(raw[b].astype(F32))
        rows = xhat.shape[0]
        g = norm_back(grad, xhat, r, gain[...])
        gfresh[b * rows : (b + 1) * rows] = g.astype(BF16)
        part_sums = row_sums([grad * xhat, grad, g.astype(BF16).astype(F32)], D)
        total = part_sums if total is None else total + part_sums
    sums[...] = total


def fresh_back(grads, raw, gain):
    batch, rows, _ = raw.shape
    flat = [g for pair in grads for g in pair]
    return pl.pallas_call(
        functools.partial(fresh_kernel, batch),
        grid=(1,),
        in_specs=[whole((rows, D)) for _ in flat] + [whole(raw.shape), whole((1, D))],
        out_specs=[whole((batch * rows, D)), whole((8, D))],
        out_shape=[
            jax.ShapeDtypeStruct((batch * rows, D), BF16),
            jax.ShapeDtypeStruct((8, D), F32),
        ],
        compiler_params=params(),
        cost_estimate=cost(2),
        name="fresh_back",
    )(*flat, raw, gain[None])


def table_kernel(keys, at, steps, w, out):
    seg = steps.shape[0] - keys
    first = pl.multiple_of((1 - at[0]) * seg, seg)
    out[...] = dot(steps[pl.ds(first, keys)], w[...], NN).astype(BF16)


def position_table(at, steps, w, keys, col, width):
    count = max(1, width // 256)
    cb = width // count
    return pl.pallas_call(
        functools.partial(table_kernel, keys),
        grid_spec=pltpu.PrefetchScalarGridSpec(
            num_scalar_prefetch=1,
            grid=(count,),
            in_specs=[
                whole(steps.shape),
                pl.BlockSpec((D, cb), lambda i, s: (0, col * count + i)),
            ],
            out_specs=pl.BlockSpec((keys, cb), lambda i, s: (0, i)),
        ),
        out_shape=jax.ShapeDtypeStruct((keys, width), BF16),
        compiler_params=params(),
        cost_estimate=cost(20),
        name="position_table",
    )(at, steps, w)


def split_out(acc, tier, rows, keep, send):
    v = acc.reshape(-1, 2, rows, acc.shape[1])
    first = tier == 0
    shape = keep.shape
    keep[...] = jnp.where(first, v[:, 0], v[:, 1]).reshape(shape).astype(BF16)
    send[...] = jnp.where(first, v[:, 1], v[:, 0]).reshape(shape).astype(BF16)


def grad_ffn_kernel(steps, n2, gpre, go, act, out):
    j = pl.program_id(0)

    @pl.when(j < steps)
    def _():
        out[...] = dot(n2[...], gpre[...], TN).astype(BF16)

    @pl.when(j >= steps)
    def _():
        out[...] = dot(go[...], act[...], TN).astype(BF16)


def grad_ffn(n2, gpre, go, act):
    rows, hidden = act.shape
    hb = min(1024, hidden)
    steps = hidden // hb

    def block(first):
        return pl.BlockSpec(
            (rows, hb), lambda j: (0, jnp.clip(j - first, 0, steps - 1))
        )

    return pl.pallas_call(
        functools.partial(grad_ffn_kernel, steps),
        grid=(2 * steps,),
        in_specs=[whole((rows, D)), block(0), whole((rows, D)), block(steps)],
        out_specs=pl.BlockSpec((D, hb), lambda j: (0, j)),
        out_shape=jax.ShapeDtypeStruct((D, 2 * hidden), BF16),
        compiler_params=params(),
        cost_estimate=cost(30),
        name="grad_ffn",
    )(n2, gpre, go, act)


def fill(y, ys):
    rows = ys[0].shape[0]
    for k, part in enumerate(ys):
        y[k * rows : (k + 1) * rows] = part[...]


def grad_kv_kernel(batch, x, *refs):
    ys, (_, out, y) = refs[:batch], refs[batch:]
    fill(y, ys)
    out[...] = dot(x[...], y[...], TN).astype(BF16)


def grad_kv(x, ys, grads, col, width):
    every = x.shape[0]
    return pl.pallas_call(
        functools.partial(grad_kv_kernel, len(ys)),
        grid=(2,),
        in_specs=[whole(x.shape)]
        + [pl.BlockSpec((y.shape[0], width), lambda j: (0, j)) for y in ys]
        + [pl.BlockSpec(memory_space=pl.ANY)],
        out_specs=pl.BlockSpec((D, width), lambda j: (0, col + j)),
        scratch_shapes=[pltpu.VMEM((every, width), BF16)],
        out_shape=jax.ShapeDtypeStruct(grads.shape, BF16),
        input_output_aliases={1 + len(ys): 0},
        compiler_params=params(),
        cost_estimate=cost(8),
        name="grad_kv",
    )(x, *ys, grads)


def grad_rest_kernel(batch, at, normed, *refs):
    gq, gbr, att = (refs[k * batch : (k + 1) * batch] for k in range(3))
    steps, gtable, out, x, y = refs[3 * batch :]
    j = pl.program_id(0)
    tier = at[0]

    @pl.when(j == 0)
    def _():
        fill(x, [normed.at[k] for k in range(batch)])
        fill(y, gq)

    @pl.when(j == 1)
    def _():
        fill(x, gbr)
        fill(y, att)

    @pl.when(j < 2)
    def _():
        out[...] = dot(x[...], y[...], TN).astype(BF16)

    @pl.when(j == 2)
    def _():
        keys = gtable.shape[1]
        seg = steps.shape[0] - keys
        first = pl.multiple_of((1 - tier) * seg, seg)
        turned = dot(gtable[...].astype(BF16), steps[pl.ds(first, keys)], NN)
        out[...] = turned.astype(BF16).T


def grad_rest(at, normed, gq, gbr, att, steps, gtable, cols):
    seg, width = gq[0].shape
    batch, local, _ = normed.shape
    return pl.pallas_call(
        functools.partial(grad_rest_kernel, batch),
        grid_spec=pltpu.PrefetchScalarGridSpec(
            num_scalar_prefetch=1,
            grid=(3,),
            in_specs=[
                pl.BlockSpec((batch, seg, D), lambda j, s: (0, local // seg - 1, 0))
            ]
            + [whole((seg, width))] * batch
            + [whole((seg, D))] * batch
            + [whole((seg, width))] * batch
            + [whole(steps.shape), whole(gtable.shape)],
            out_specs=pl.BlockSpec((D, width), lambda j, s: (0, j)),
            scratch_shapes=[
                pltpu.VMEM((batch * seg, D), BF16),
                pltpu.VMEM((batch * seg, width), BF16),
            ],
        ),
        out_shape=jax.ShapeDtypeStruct((D, cols), BF16),
        compiler_params=params(),
        cost_estimate=cost(8),
        name="grad_rest",
    )(at, normed, *gq, *gbr, *att, steps, gtable)


def grad_conv_kernel(rows, at, taps, fresh, keep, send):
    split_out(dot(taps[...], fresh[...], TN), at[0], rows, keep, send)


def grad_conv(at, grouped, fresh, wide, rows):
    count = grouped.shape[0]
    return pl.pallas_call(
        functools.partial(grad_conv_kernel, rows),
        grid_spec=pltpu.PrefetchScalarGridSpec(
            num_scalar_prefetch=1,
            grid=(KW,),
            in_specs=[
                pl.BlockSpec((count, D), lambda j, s: (0, j)),
                pl.BlockSpec((count, wide), lambda j, s: (0, s[1])),
            ],
            out_specs=[pl.BlockSpec((D // 2, wide), lambda j, s: (0, j))] * 2,
        ),
        out_shape=[jax.ShapeDtypeStruct((D // 2, KW * wide), BF16)] * 2,
        compiler_params=params(),
        cost_estimate=cost(4),
        name="grad_conv",
    )(at, grouped, fresh)


def conv_kernel(taps, w, bias, out):
    k = pl.program_id(0)
    part = dot(taps[...], w[...], NN)

    @pl.when(k == 0)
    def _():
        out[...] = part + bias[...]

    @pl.when(k > 0)
    def _():
        out[...] += part


def compress(grouped, w, bias):
    count = grouped.shape[0]
    wide = bias.shape[0]
    return pl.pallas_call(
        conv_kernel,
        grid=(KW,),
        in_specs=[
            pl.BlockSpec((count, D), lambda j: (0, j)),
            pl.BlockSpec((D, wide), lambda j: (0, j)),
            whole((1, wide)),
        ],
        out_specs=whole((count, wide)),
        out_shape=jax.ShapeDtypeStruct((count, wide), F32),
        compiler_params=params(),
        cost_estimate=cost(3),
        name="compress",
    )(grouped, w, bias[None])


def distance_rows(first, count):
    half = D // 2
    freq = np.exp(np.arange(half) * (-2.0 * math.log(10000.0) / D))
    turned = (first - np.arange(count))[:, None] * freq[None, :]
    return np.concatenate([np.sin(turned), np.cos(turned)], axis=1).astype(
        ml_dtypes.bfloat16
    )


def col_sum(x):
    return jnp.sum(x, axis=tuple(range(x.ndim - 1)))


def ein(spec, a, b):
    return jnp.einsum(spec, a, b, preferred_element_type=F32)


def norm_rows(rows, gain, shift):
    return (standardize(rows.astype(F32))[0] * gain + shift).astype(BF16)


def shards(
    segment_input,
    memory,
    compressed,
    evicted,
    cotangent,
    seg_lengths,
    memory_fills,
    compressed_fills,
    conv_weight,
    conv_bias,
    norm1_gain,
    norm1_bias,
    query_weight,
    key_weight,
    value_weight,
    position_weight,
    content_bias,
    position_bias,
    out_weight,
    norm2_gain,
    norm2_bias,
    up_weight,
    up_bias,
    down_weight,
    down_bias,
):
    tier = lax.axis_index("tier")
    head = lax.axis_index("head")
    heads_n = lax.axis_size("head")
    batch, seg, _ = segment_input.shape
    mem = memory.shape[1]
    comp = compressed.shape[1]
    fresh = evicted.shape[1] // KW
    sizes = (comp, fresh, mem, seg)
    width = query_weight.shape[1]
    wide = conv_weight.shape[2]
    hidden = up_weight.shape[1]
    keys = 2 * (comp + fresh + mem + seg)
    rows = query_weight.shape[0]
    streams = range(batch)
    at = jnp.concatenate(
        [
            jnp.stack([tier, head]).astype(jnp.int32),
            jnp.stack([compressed_fills, memory_fills, seg_lengths], 1).reshape(-1),
        ]
    )


    conv_z = gather_z(jnp.concatenate([conv_weight[k] for k in range(KW)], 1))
    out_t = head_gather(out_weight.T)
    full = out_t.shape[1]
    attn_pack = jnp.concatenate(
        [key_weight, value_weight, query_weight, position_weight], 1
    )
    ffn_pack = jnp.concatenate([out_t, up_weight, down_weight.T], 1)
    attn_z = gather_z(after(attn_pack, conv_z, out_t))
    ffn_w = lax.all_gather(
        after(ffn_pack, conv_z), ("dp", "tier"), axis=0, tiled=True
    )
    conv_blocks = gather_yt(conv_z)
    conv_blocks[0] = after(conv_blocks[0], out_t)
    conv_w = place(conv_blocks)

    n_comp = norm_rows(compressed, norm1_gain, norm1_bias)
    n_mem = norm_rows(memory, norm1_gain, norm1_bias)
    n_seg = norm_rows(segment_input, norm1_gain, norm1_bias)
    grouped = evicted.reshape(batch * fresh, KW * D)
    fresh_part = compress(grouped, conv_w, conv_bias).astype(BF16)
    fresh_rows = head_gather(fresh_part.reshape(batch, fresh, wide))
    n_fresh = norm_rows(fresh_rows, norm1_gain, norm1_bias)
    attn_blocks = gather_yt(attn_z)
    attn_blocks[0] = after(attn_blocks[0], fresh_part)
    attn_w = place(attn_blocks)

    normed, kv, q = project(n_comp, n_fresh, n_mem, n_seg, attn_w)
    kv_other = swap(kv, "tier")
    steps = jnp.asarray(distance_rows(keys - 1, keys + seg))
    table = position_table(at, steps, after(attn_w, kv), keys, 3, width)
    atts, probs, others = [], [], []
    for b in streams:
        q_b = after(q, *(others[-2:-1] + atts[-1:])) if b else after(q, table)
        att, p = attend(
            b, at, q_b, kv, kv_other, table, content_bias, position_bias, sizes
        )
        atts.append(att)
        probs.append(p)
        if heads_n == 2:
            others.append(swap(att, "head"))
        else:
            others.append(lax.all_gather(att, "head", axis=1, tiled=True))

    def over_head(x):
        if heads_n == 2:
            return [x, swap(x, "head")]
        return [lax.psum(x, "head")]

    if heads_n == 2:
        pairs = [v for pair in zip(atts, others) for v in pair]
    else:
        pairs = others
    hid, n2, go, act, gpre, up_sums, out_sums, *halves = feed_forward(
        at,
        pairs,
        segment_input,
        cotangent,
        ffn_w,
        full,
        norm2_gain,
        norm2_bias,
        up_bias,
    )
    twos = [over_head(halves[0])]
    g_ffn = grad_ffn(n2, gpre, go, act)
    g_ffn_s = lax.psum_scatter(
        g_ffn, ("dp", "tier"), scatter_dimension=0, tiled=True
    )

    ghids, gbrs, gqs, keeps, gots = [], [], [], [], []
    gkvs, parts, fparts, downs = [], [], [], []
    bias_sums, mem_sums, mid_rows = 0, 0, 0
    gtable = None
    last = g_ffn

    def rows_of(b, *others):
        gq = after(gqs[b], *others)
        gkv, part, fpart, sums = rows_back(
            b, keeps[b], gots[b], gq, n_mem, attn_w, sizes
        )
        gkvs.append(gkv)
        fparts.append(over_head(fpart))
        parts.append(over_head(part) if b == 0 else part)
        return sums[:2], part

    for b in streams:
        if b > 1:
            sums, last = rows_of(b - 2, last)
            mem_sums = mem_sums + sums
        if b < batch - 1:
            twos.append(over_head(after(halves[b + 1], twos[b][-1])))
        ghid, gbr, sums, gq, keep, send, gtable, gbias = attend_back(
            b,
            at,
            twos[b],
            hid,
            after(go, last),
            norm2_gain,
            ffn_w,
            probs[b],
            q,
            kv,
            kv_other,
            table,
            content_bias,
            position_bias,
            sizes,
            gtable,
        )
        last = gq
        ghids.append(ghid)
        gbrs.append(gbr)
        gqs.append(gq)
        keeps.append(keep)
        gots.append(swap(send, "tier"))
        if 0 < b:
            downs.append(over_head(after(halves[batch + b - 1], gq)))
        mid_rows = mid_rows + sums
        bias_sums = bias_sums + gbias
    for b in range(max(batch - 2, 0), batch):
        sums, last = rows_of(b, last)
        mem_sums = mem_sums + sums
    early = [pair[-1] for pair in fparts[:-1]]
    gq_0 = after(gqs[0], last, parts[0][-1], *early)
    grads = grad_rest(
        at, normed, [gq_0] + gqs[1:], gbrs, atts, steps, gtable, 5 * width
    )
    for b in range(1, batch):
        parts[b] = over_head(after(parts[b], fparts[-1][-1]))
    fresh_grad, fresh_sums = fresh_back(
        fparts, after(fresh_rows, grads), norm1_gain
    )
    keep, send = grad_conv(at, grouped, fresh_grad, wide, rows)
    grads = grad_kv(after(normed, keep, g_ffn_s).reshape(-1, D), gkvs, grads, 3, width)
    grads_s = lax.psum_scatter(
        grads, ("dp", "tier"), scatter_dimension=0, tiled=True
    )
    got = swap(send, "tier")
    row_totals = fresh_sums[:2]
    before = None

    def context_of(b, *others):
        return context_back(
            b,
            parts[b],
            compressed,
            segment_input,
            after(ghids[b], *others),
            norm1_gain,
            before,
            sizes,
        )

    mine, theirs = halve(keep, after(got, grads))
    other = swap(theirs, "dp")
    *before, sums = context_of(0, theirs)
    row_totals = row_totals + sums[:2]
    added = add_low(mine, other)
    conv_all = z_exchange(added)
    for b in range(1, batch):
        *before, sums = context_of(
            b, before[1], conv_all if b == batch - 1 else added
        )
        row_totals = row_totals + sums[:2]
    grad_comp, grad_in = before
    g_conv = jnp.sum(after(conv_all, grad_in).astype(F32), axis=0)
    g_conv = jnp.stack([g_conv[:, k * wide : (k + 1) * wide] for k in range(KW)])
    mem_sums = sum(over_head(after(mem_sums, grad_in)))
    downs.append(over_head(after(halves[-1], grad_in)))
    grads_s = after(grads_s, conv_all)
    g_q, g_out, g_pos, g_k, g_v = (
        grads_s[:, k * width : (k + 1) * width].astype(F32) for k in range(5)
    )

    outs = []
    for b in streams:
        out = hid[b * seg : (b + 1) * seg] + down_bias
        for x in downs[b]:
            out = out + x.astype(F32)
        outs.append(out.astype(BF16))
    output = jnp.stack(outs)
    mem_gain = (mem_sums[0] - norm1_bias * mem_sums[1]) / norm1_gain
    fresh_sum = lax.dynamic_slice_in_dim(fresh_sums[2], head * wide, wide, 0)
    sums = small_sum(
        [
            mid_rows[0],
            mid_rows[1],
            up_sums[0],
            out_sums[0],
            fresh_sum,
            row_totals[0] + mem_gain,
            row_totals[1] + mem_sums[1],
            bias_sums[:, 0],
            bias_sums[:, 1],
        ]
    )
    return (
        output,
        grad_in,
        grad_comp,
        g_conv,
        sums[4],
        sums[5],
        sums[6],
        g_q,
        g_k,
        g_v,
        g_pos,
        sums[7],
        sums[8],
        g_out.T,
        sums[0],
        sums[1],
        g_ffn_s[:, :hidden].astype(F32),
        sums[2],
        g_ffn_s[:, hidden:].T.astype(F32),
        sums[3],
    )


def solution(mesh):
    rows = P("dp", "tier", None)
    by_row = P(("dp", "tier"), "head")
    by_col = P("head", ("dp", "tier"))
    conv = P(None, ("dp", "tier"), "head")
    heads = P("head", None)
    placed = (
        (rows,) * 5
        + (P("dp"),) * 3
        + (conv, P("head"), P(), P())
        + (by_row,) * 4
        + (heads, heads, by_col, P(), P(), by_row, P("head"), by_col, P())
    )
    results = (
        (rows,) * 3
        + (conv, P("head"), P(), P())
        + (by_row,) * 4
        + (heads, heads, by_col, P(), P(), by_row, P("head"), by_col, P())
    )
    return jax.shard_map(
        shards, mesh=mesh, in_specs=placed, out_specs=results, check_vma=False
    )
```
